128 devices in a mesh: node: 8 (over y, core), group: 16 (over x, z).
Axes of the slice: x: 4, y: 4, z: 4, core: 2. Of those that a mesh axis runs over, the one named last changes fastest.
Arguments:
- queries: bfloat16 [512, 8192], P('group'), may hold values from -12 to 12
- new_entry: bfloat16 [512, 2048], P('group'), may hold values from -8 to 8
- block_lists: int32 [512, 64], P('group'), may hold values from 0 to 6143, as said below
- list_lengths: int32 [512], P('group'), may hold values from 61 to 64, as said below
- block_fill: int32 [6144], P(('node', 'group')), may hold values from 1 to 16
- cache_pool: bfloat16 [6144, 16, 2048], P(('node', 'group')), may hold values from -3.5 to 3.5
Outputs:
- attended: bfloat16 [512, 8192], P('group')
The draws below stay inside these ranges and needn't reach their ends.
Inputs may be any that keep to these rules, and one draw needn't show every extreme that they name: `block_lists`: each rollout's list holds 40 blocks shared by all rollouts, then 20 blocks of one of 8 branches, then 4 blocks of its own; no id repeats within a list. `list_lengths`: entries of a list at or past its length are ignored.
All inputs are finite; a program needn't handle non-finite values.
Results may differ from the reference program's by a relative error of at most 0.0095.
Values may be sent and summed in bfloat16 or wider, within the bound.
No kernel may reach another device: no remote copies, remote signals or barrier semaphores. Data moves between devices by JAX's collectives and lax.ppermute only.
A program may use at most 128 MiB of HBM per device.

```python
import math
import jax
import jax.numpy as jnp
from jax import lax

HEADS = 64
KV_HEADS = 8
HEAD_DIM = 128
BLK_TOKENS = 16
ROOT_BLOCKS = 40
BRANCHES = 8
BRANCH_BLOCKS = 20
PRIVATE_BLOCKS = 4
LIST = 64
ROLLOUTS = 512
POOL_BLOCKS = 6144


def tree_lists(key):
    perm = jax.random.permutation(jax.random.fold_in(key, 201), POOL_BLOCKS).astype(jnp.int32)
    spot = jnp.argmax(perm == POOL_BLOCKS - 1)
    perm = jnp.roll(perm, -spot)
    root = perm[:ROOT_BLOCKS]
    branch_start = ROOT_BLOCKS
    branch_ids = perm[branch_start:branch_start + BRANCHES * BRANCH_BLOCKS].reshape(BRANCHES, BRANCH_BLOCKS)
    own_start = branch_start + BRANCHES * BRANCH_BLOCKS
    private = perm[own_start:own_start + ROLLOUTS * PRIVATE_BLOCKS].reshape(ROLLOUTS, PRIVATE_BLOCKS)
    picked = jax.random.randint(jax.random.fold_in(key, 202), (ROLLOUTS,), 0, BRANCHES)
    lists = jnp.concatenate([jnp.broadcast_to(root[None, :], (ROLLOUTS, ROOT_BLOCKS)), branch_ids[picked], private], axis=1)
    extra = jax.random.randint(jax.random.fold_in(key, 203), (ROLLOUTS,), 1, PRIVATE_BLOCKS + 1)
    lengths = (ROOT_BLOCKS + BRANCH_BLOCKS + extra).astype(jnp.int32)
    lengths = lengths.at[0].set(LIST)
    return (lists.astype(jnp.int32), lengths.astype(jnp.int32))


def draw_block_lists(key, part):
    return tree_lists(key)[0]


def draw_list_lengths(key, part):
    return tree_lists(key)[1]


def draw_block_fill(key, part):
    key = jax.random.fold_in(key, 3)
    partial_pick = jax.random.randint(jax.random.fold_in(key, 1), (POOL_BLOCKS,), 0, 3)
    partial_fill = jax.random.randint(jax.random.fold_in(key, 2), (POOL_BLOCKS,), 1, BLK_TOKENS + 1)
    return jnp.where(partial_pick == 0, partial_fill, BLK_TOKENS).astype(jnp.int32)


def draw_queries(key, part):
    key = jax.random.fold_in(key, 5)
    shape = (ROLLOUTS, HEADS * HEAD_DIM)
    values = jnp.clip(jax.random.normal(key, shape, jnp.float32), -6.0, 6.0)
    return values.astype(jnp.bfloat16)


def draw_cache_pool(key, part):
    key = jax.random.fold_in(key, 7)
    shape = (POOL_BLOCKS, BLK_TOKENS, 2 * KV_HEADS * HEAD_DIM)
    values = jnp.clip(jax.random.normal(key, shape, jnp.float32), -3.5, 3.5)
    return values.astype(jnp.bfloat16)


def steps_of(key, dims, pieces, low, high):
    level = 1.0
    for dim, shards_of in pieces:
        heights = jax.random.uniform(jax.random.fold_in(jax.random.fold_in(key, 6), dim), (shards_of,), jnp.float32, low / len(pieces), high / len(pieces))
        level = level * jnp.repeat(jnp.exp(heights), dims[dim] // shards_of).reshape((-1,) + (1,) * (len(dims) - 1 - dim))
    return level


def noise(rng, shape, scale, bound, pieces=(), held_as=jnp.bfloat16):
    factor_of = steps_of(rng, shape, pieces, -0.22, 0.18) if pieces else 1.0
    values = jax.random.normal(rng, shape, jnp.float32) * scale * factor_of
    return jnp.minimum(jnp.maximum(values, -bound), bound).astype(held_as)


def setup_inputs(seed: int = 0) -> dict:
    arg_keys = jax.random.split(jax.random.key(seed), 7)
    return {
        "queries": draw_queries(jax.random.fold_in(arg_keys[6], 71), 0),
        "new_entry": noise(arg_keys[1], (ROLLOUTS, 2 * KV_HEADS * HEAD_DIM), 2.0, 8.0, ((0, 16),)),
        "block_lists": draw_block_lists(jax.random.fold_in(arg_keys[6], 71), 0),
        "list_lengths": draw_list_lengths(jax.random.fold_in(arg_keys[6], 71), 0),
        "block_fill": draw_block_fill(jax.random.fold_in(arg_keys[6], 71), 0),
        "cache_pool": draw_cache_pool(jax.random.fold_in(arg_keys[6], 71), 0),
    }


def reference(queries, new_entry, block_lists, list_lengths, block_fill, cache_pool):
    width = KV_HEADS * HEAD_DIM
    group_size = HEADS // KV_HEADS
    scale = 1.0 / math.sqrt(HEAD_DIM)
    positions = jnp.arange(BLK_TOKENS, dtype=jnp.int32)
    entries = jnp.arange(LIST, dtype=jnp.int32)

    def one_rollout(items):
        query, entry, blocks, length = items
        gathered = cache_pool[blocks.astype(jnp.int32)]
        fills = block_fill[blocks.astype(jnp.int32)]
        visible = (entries[:, None] < length) & (positions[None, :] < fills[:, None])
        visible = visible.reshape(LIST * BLK_TOKENS)
        flat = gathered.reshape(LIST * BLK_TOKENS, 2 * width)
        keys = flat[:, :width].astype(jnp.float32).reshape(-1, KV_HEADS, HEAD_DIM)
        values = flat[:, width:].astype(jnp.float32).reshape(-1, KV_HEADS, HEAD_DIM)
        grouped = query.astype(jnp.float32).reshape(KV_HEADS, group_size, HEAD_DIM)
        scores = jnp.einsum('hgd,thd->hgt', grouped, keys) * scale
        own_entry = entry.astype(jnp.float32)
        own_key = own_entry[:width].reshape(KV_HEADS, HEAD_DIM)
        own_value = own_entry[width:].reshape(KV_HEADS, 1, HEAD_DIM)
        own = jnp.einsum('hgd,hd->hg', grouped, own_key) * scale
        peak = jnp.maximum(lax.optimization_barrier(jnp.max(jnp.where(visible[None, None, :], scores, -1e+30), axis=-1)), own)
        weights = jnp.where(visible[None, None, :], jnp.exp(scores - peak[..., None]), 0.0)
        own_weight = jnp.exp(own - peak)
        total = lax.optimization_barrier(jnp.sum(weights, axis=-1)) + own_weight
        rounded = lax.optimization_barrier(weights.astype(jnp.bfloat16)).astype(jnp.float32)
        accum = jnp.einsum('hgt,thd->hgd', rounded, values) + own_weight[..., None] * own_value
        return (accum / total[..., None]).reshape(HEADS * HEAD_DIM).astype(jnp.bfloat16)
    return lax.map(one_rollout, (queries, new_entry, block_lists, list_lengths))
```

```python
import functools
import math

import jax
import jax.numpy as jnp
from jax import lax
from jax.experimental import pallas as pl
from jax.experimental.pallas import tpu as pltpu
from jax.sharding import PartitionSpec as P

HEADS = 64
KV_HEADS = 8
HEAD_DIM = 128
BLK_TOKENS = 16
ROOT_BLOCKS = 40
LIST = 64
WIDTH = KV_HEADS * HEAD_DIM
GROUP = HEADS // KV_HEADS
SCALE = 1.0 / math.sqrt(HEAD_DIM)

HOLDERS = 8
OWN_BLOCKS = 48
BLOCKS = HOLDERS * OWN_BLOCKS
PIECE_ROWS = OWN_BLOCKS * BLK_TOKENS + OWN_BLOCKS
TILE = 64
CHUNK = 16
ROWS = TILE * GROUP
TOKENS = CHUNK * BLK_TOKENS
OUT_ROWS = 32 * GROUP + 16
LOW = -1e9
DEAD = -1e30


def attend_kernel(codes, counts, kv, query, lists, out, fills, keys, values, scores):
    for source in range(HOLDERS):
        base = source * PIECE_ROWS + OWN_BLOCKS * BLK_TOKENS
        fills[pl.ds(source * OWN_BLOCKS, OWN_BLOCKS), :] = kv[
            pl.ds(base, OWN_BLOCKS), 0:HEAD_DIM
        ].astype(jnp.float32)
    values[:, HEAD_DIM:] = jnp.ones((TOKENS, HEAD_DIM), jnp.bfloat16)
    row_rollout = lax.broadcasted_iota(jnp.int32, (ROWS, HEAD_DIM), 0) // GROUP
    lane = lax.broadcasted_iota(jnp.int32, (ROWS, HEAD_DIM), 1)
    member_lanes = jnp.where(row_rollout == lane, 1.0, 0.0).astype(jnp.bfloat16)
    token = lax.broadcasted_iota(jnp.int32, (BLK_TOKENS, HEAD_DIM), 0).astype(jnp.float32)
    pick = lax.broadcasted_iota(jnp.int32, (8, HEAD_DIM), 0)
    pick_lane = lax.broadcasted_iota(jnp.int32, (8, HEAD_DIM), 1)
    picked = jnp.where(pick == pick_lane, 1.0, 0.0).astype(jnp.bfloat16)

    def start_row(block):
        source = (block * 1366) >> 16
        return pl.multiple_of(block * BLK_TOKENS + source * OWN_BLOCKS, BLK_TOKENS)

    def one_tile(tile, _):
        chunks = (counts[tile] + CHUNK - 1) // CHUNK
        rows = query[pl.ds(pl.multiple_of(tile * ROWS, ROWS), ROWS), :]
        left = jnp.concatenate([rows, member_lanes], axis=1)
        listed = lists[tile]

        def first_pass(chunk, highest):
            for slot in range(CHUNK):
                code = codes[tile * BLOCKS + chunk * CHUNK + slot]
                block = jnp.maximum(code, 0)
                row = start_row(block)
                place = pl.ds(slot * BLK_TOKENS, BLK_TOKENS)
                keys[place, 0:HEAD_DIM] = kv[pl.ds(row, BLK_TOKENS), 0:HEAD_DIM]
                member = jnp.max(
                    jnp.where(listed == code, 1.0, 0.0), axis=0, keepdims=True
                )
                live = (token < fills[pl.ds(block, 1), :]) & (member > 0.5)
                keys[place, HEAD_DIM:] = jnp.where(live, 0.0, DEAD).astype(jnp.bfloat16)
            found = lax.dot_general(
                left, keys[...], (((1,), (1,)), ((), ())), preferred_element_type=jnp.float32
            )
            scores[chunk] = found
            return jnp.maximum(highest, jnp.maximum(found[:, :HEAD_DIM], found[:, HEAD_DIM:]))

        highest = lax.fori_loop(
            0, chunks, first_pass, jnp.full((ROWS, HEAD_DIM), DEAD, jnp.float32)
        )
        peak = jnp.maximum(jnp.max(highest, axis=1, keepdims=True) * SCALE, LOW)
        peak = peak.astype(jnp.bfloat16).astype(jnp.float32)

        def second_pass(chunk, accum):
            for slot in range(CHUNK):
                code = codes[tile * BLOCKS + chunk * CHUNK + slot]
                row = start_row(jnp.maximum(code, 0))
                values[pl.ds(slot * BLK_TOKENS, BLK_TOKENS), 0:HEAD_DIM] = kv[
                    pl.ds(row, BLK_TOKENS), HEAD_DIM:
                ]
            weights = jnp.exp(scores[chunk] * SCALE - peak).astype(jnp.bfloat16)
            return accum + jnp.dot(weights, values[...], preferred_element_type=jnp.float32)

        accum = lax.fori_loop(
            0, chunks, second_pass, jnp.zeros((ROWS, 2 * HEAD_DIM), jnp.float32)
        )
        total = accum[:, HEAD_DIM:]
        coarse = total.astype(jnp.bfloat16).astype(jnp.float32)
        stats = jnp.where(lane == 0, peak, jnp.where(lane == 1, coarse, total - coarse))
        flat = lax.dot_general(
            picked,
            stats.astype(jnp.bfloat16),
            (((1,), (1,)), ((), ())),
            preferred_element_type=jnp.float32,
        )
        for part in range(TILE // 32):
            count = 32 * GROUP
            out[tile * (TILE // 32) + part, 0:count, :] = accum[
                part * count : (part + 1) * count, :HEAD_DIM
            ].astype(jnp.bfloat16)
            both = jnp.concatenate(
                [
                    flat[:, part * count : part * count + HEAD_DIM],
                    flat[:, part * count + HEAD_DIM : (part + 1) * count],
                ],
                axis=0,
            )
            out[tile * (TILE // 32) + part, count:, :] = both.astype(jnp.bfloat16)
        return 0

    lax.fori_loop(0, counts.shape[0], one_tile, 0)


def attend(codes, counts, kv, query, lists):
    vmem = pl.BlockSpec(memory_space=pltpu.VMEM)
    smem = pl.BlockSpec(memory_space=pltpu.SMEM)
    sources = query.shape[0] // (32 * GROUP)
    return pl.pallas_call(
        attend_kernel,
        out_shape=jax.ShapeDtypeStruct((sources, OUT_ROWS, HEAD_DIM), jnp.bfloat16),
        in_specs=[smem, smem, vmem, vmem, vmem],
        out_specs=vmem,
        scratch_shapes=[
            pltpu.VMEM((BLOCKS, HEAD_DIM), jnp.float32),
            pltpu.VMEM((TOKENS, 2 * HEAD_DIM), jnp.bfloat16),
            pltpu.VMEM((TOKENS, 2 * HEAD_DIM), jnp.bfloat16),
            pltpu.VMEM((BLOCKS // CHUNK, ROWS, TOKENS), jnp.float32),
        ],
        compiler_params=pltpu.CompilerParams(vmem_limit_bytes=50 * 1024 * 1024),
        cost_estimate=pl.CostEstimate(
            flops=4 * 4096 * 512 * 256, bytes_accessed=6 << 20, transcendentals=4096 * 512
        ),
        name="attend",
    )(codes, counts, kv, query, lists)


def finish_kernel(parts, query, entry, out, peaks, totals):
    sources = parts.shape[0]
    count = parts.shape[1] - 16
    which = lax.broadcasted_iota(jnp.int32, (8, 2 * HEAD_DIM), 0)
    lane = lax.broadcasted_iota(jnp.int32, (8, 2 * HEAD_DIM), 1)
    spread = jnp.where(
        lane < HEAD_DIM, jnp.where(which == 0, 1.0, 0.0), jnp.where((which == 1) | (which == 2), 1.0, 0.0)
    ).astype(jnp.bfloat16)
    rollouts = count // GROUP
    own_key = jnp.broadcast_to(
        entry[:, 0:HEAD_DIM].astype(jnp.float32)[:, None, :], (rollouts, GROUP, HEAD_DIM)
    ).reshape(count, HEAD_DIM)
    own_value = jnp.broadcast_to(
        entry[:, HEAD_DIM:].astype(jnp.float32)[:, None, :], (rollouts, GROUP, HEAD_DIM)
    ).reshape(count, HEAD_DIM)
    own = jnp.sum(query[...].astype(jnp.float32) * own_key, axis=1, keepdims=True) * SCALE
    highest = jnp.broadcast_to(own, (count, HEAD_DIM))
    for source in range(sources):
        flat = parts[source, count:, :].astype(jnp.float32)
        for half in range(count // HEAD_DIM):
            wide = lax.dot_general(
                flat[half * 8 : half * 8 + 8, :].astype(jnp.bfloat16),
                spread,
                (((0,), (0,)), ((), ())),
                preferred_element_type=jnp.float32,
            )
            place = pl.ds(half * HEAD_DIM, HEAD_DIM)
            peaks[source, place, :] = wide[:, :HEAD_DIM]
            totals[source, place, :] = wide[:, HEAD_DIM:]
        highest = jnp.maximum(highest, peaks[source])
    weight = jnp.exp(own - highest)
    total = weight
    accum = weight * own_value
    for source in range(sources):
        weight = jnp.exp(peaks[source] - highest)
        total = total + weight * totals[source]
        accum = accum + weight * parts[source, 0:count, :].astype(jnp.float32)
    out[...] = (accum / total).astype(jnp.bfloat16)


def finish(parts, query, entry):
    count = query.shape[0]
    vmem = pl.BlockSpec(memory_space=pltpu.VMEM)
    return pl.pallas_call(
        finish_kernel,
        out_shape=jax.ShapeDtypeStruct((count, HEAD_DIM), jnp.bfloat16),
        in_specs=[vmem, vmem, vmem],
        out_specs=vmem,
        scratch_shapes=[
            pltpu.VMEM((parts.shape[0], count, HEAD_DIM), jnp.float32),
            pltpu.VMEM((parts.shape[0], count, HEAD_DIM), jnp.float32),
        ],
        compiler_params=pltpu.CompilerParams(vmem_limit_bytes=50 * 1024 * 1024),
        name="finish",
    )(parts, query, entry)


def local_number(ids, column):
    device = ids // OWN_BLOCKS
    here = (device % 16) == column
    return jnp.where(here, (device // 16) * OWN_BLOCKS + ids % OWN_BLOCKS, -1)


def visits(root, lists):
    tiles = lists.shape[0]
    numbers = jnp.arange(BLOCKS, dtype=jnp.int32)
    hit = jnp.any(lists[:, :, None] == numbers, axis=1)
    hit = hit | jnp.any(root[:, None] == numbers, axis=0)[None, :]
    counts = jnp.sum(hit, axis=1, dtype=jnp.int32)
    before = (numbers[:, None] < numbers[None, :]).astype(jnp.bfloat16)
    place = jnp.dot(hit.astype(jnp.bfloat16), before, preferred_element_type=jnp.float32)
    place = jnp.where(hit, place.astype(jnp.int32), -1)
    codes = jnp.sum(
        jnp.where(place[:, None, :] == numbers[None, :, None], numbers + 2, 0), axis=2
    )
    return (codes - 2).astype(jnp.int32).reshape(tiles * BLOCKS), counts


def per_device(queries, new_entry, block_lists, list_lengths, block_fill, cache_pool):
    node = lax.axis_index("node")
    column = lax.axis_index("group")
    groups = lax.axis_size("group")
    own_rows = queries.shape[0]

    by_head = cache_pool.reshape(OWN_BLOCKS * BLK_TOKENS, 2, KV_HEADS, HEAD_DIM)
    by_head = jnp.transpose(by_head, (2, 0, 1, 3)).reshape(
        KV_HEADS, OWN_BLOCKS * BLK_TOKENS, 2 * HEAD_DIM
    )
    fill_rows = jnp.broadcast_to(
        block_fill.astype(jnp.bfloat16)[None, :, None], (KV_HEADS, OWN_BLOCKS, 2 * HEAD_DIM)
    )
    sent = jnp.concatenate([by_head, fill_rows], axis=1)
    kv = lax.all_to_all(sent, "node", split_axis=0, concat_axis=0, tiled=True)
    kv = kv.reshape(HOLDERS * PIECE_ROWS, 2 * HEAD_DIM)

    head_query = lax.dynamic_slice_in_dim(queries, node * WIDTH, WIDTH, axis=1)
    entries = jnp.arange(LIST, dtype=jnp.int32)[None, :]
    tail = jnp.where(entries < list_lengths[:, None], block_lists, 8191)[:, ROOT_BLOCKS:]
    coded = jnp.concatenate([tail // 128, tail % 128], axis=1).astype(jnp.bfloat16)
    coded = jnp.pad(coded, ((0, 0), (0, HEAD_DIM - coded.shape[1])))
    told = jnp.concatenate([head_query, coded], axis=1)
    told = lax.all_to_all(
        jnp.broadcast_to(told[None], (groups,) + told.shape),
        "group",
        split_axis=0,
        concat_axis=0,
        tiled=True,
    )
    all_query = told[:, :, :WIDTH].reshape(groups * own_rows * GROUP, HEAD_DIM)
    coded = told[:, :, WIDTH:].astype(jnp.int32).reshape(groups * own_rows, HEAD_DIM)
    count = LIST - ROOT_BLOCKS
    ids = coded[:, :count] * 128 + coded[:, count : 2 * count]
    tail = jnp.where(ids < 8191, local_number(ids, column), -1)
    root = local_number(block_lists[0, :ROOT_BLOCKS], column)
    tiles = groups * own_rows // TILE
    codes, counts = visits(root, tail.reshape(tiles, TILE * count))
    listed = jnp.concatenate(
        [
            jnp.broadcast_to(root[None, :, None], (tiles, ROOT_BLOCKS, TILE)),
            jnp.transpose(tail.reshape(tiles, TILE, count), (0, 2, 1)),
        ],
        axis=1,
    )
    listed = jnp.pad(listed, ((0, 0), (0, 0), (0, HEAD_DIM - TILE)), constant_values=-1)

    partial = attend(codes, counts, kv, all_query, listed)
    parts = lax.all_to_all(partial, "group", split_axis=0, concat_axis=0, tiled=True)
    key = lax.dynamic_slice_in_dim(new_entry, node * HEAD_DIM, HEAD_DIM, axis=1)
    value = lax.dynamic_slice_in_dim(new_entry, WIDTH + node * HEAD_DIM, HEAD_DIM, axis=1)
    done = finish(
        parts,
        head_query.reshape(own_rows * GROUP, HEAD_DIM),
        jnp.concatenate([key, value], axis=1),
    )
    gathered = lax.all_gather(done.reshape(own_rows, WIDTH), "node")
    return jnp.transpose(gathered, (1, 0, 2)).reshape(own_rows, HEADS * HEAD_DIM)


def solution(mesh):
    return jax.shard_map(
        per_device,
        mesh=mesh,
        in_specs=(
            P("group", None),
            P("group", None),
            P("group", None),
            P("group"),
            P(("node", "group")),
            P(("node", "group"), None, None),
        ),
        out_specs=P("group", None),
        check_vma=False,
    )
```

```python
import functools
import math

import jax
import jax.numpy as jnp
from jax import lax
from jax.experimental import pallas as pl
from jax.experimental.pallas import tpu as pltpu
from jax.sharding import PartitionSpec as P

HEADS = 64
KV_HEADS = 8
HEAD_DIM = 128
BLK_TOKENS = 16
ROOT_BLOCKS = 40
LIST = 64
WIDTH = KV_HEADS * HEAD_DIM
GROUP = HEADS // KV_HEADS
SCALE = 1.0 / math.sqrt(HEAD_DIM)

HOLDERS = 8
OWN_BLOCKS = 48
BLOCKS = HOLDERS * OWN_BLOCKS
FILL_ROWS = 16
PIECE_ROWS = OWN_BLOCKS * BLK_TOKENS + FILL_ROWS
TILE = 64
CHUNK = 32
ROWS = TILE * GROUP
PACK_PARTS = 4
TOGETHER = 2
TOKENS = CHUNK * BLK_TOKENS
OUT_ROWS = 32 * GROUP + 16
LOW = -1e9
DEAD = -1e30


def pack_kernel(fill, pool, out, staged, fill_rows, arrived, left):
    tokens = OWN_BLOCKS * BLK_TOKENS
    span = tokens // PACK_PARTS

    def fetch(part):
        place = pl.ds(part * span, span)
        return pltpu.make_async_copy(pool.at[place, :], staged.at[place, :], arrived.at[part])

    def send(part, head, half):
        place = pl.ds(part * span, span)
        return pltpu.make_async_copy(
            staged.at[place, pl.ds((half * KV_HEADS + head) * HEAD_DIM, HEAD_DIM)],
            out.at[head, place, pl.ds(half * HEAD_DIM, HEAD_DIM)],
            left.at[(part * KV_HEADS + head) * 2 + half],
        )

    def send_fill(head):
        return pltpu.make_async_copy(
            fill_rows,
            out.at[head, pl.ds(tokens, FILL_ROWS), :],
            left.at[PACK_PARTS * KV_HEADS * 2 + head],
        )

    for part in range(PACK_PARTS):
        fetch(part).start()
    row = lax.broadcasted_iota(jnp.int32, (FILL_ROWS, 2 * HEAD_DIM), 0)
    part_of = lax.broadcasted_iota(jnp.int32, (FILL_ROWS, 2 * HEAD_DIM), 1) // 64
    number = part_of * FILL_ROWS + row
    filled = jnp.zeros((FILL_ROWS, 2 * HEAD_DIM), jnp.int32)
    for block in range(OWN_BLOCKS):
        filled = jnp.where(number == block, fill[block], filled)
    fill_rows[...] = filled.astype(jnp.float32).astype(jnp.bfloat16)
    for head in range(KV_HEADS):
        send_fill(head).start()
    for part in range(PACK_PARTS):
        fetch(part).wait()
        for head in range(KV_HEADS):
            for half in range(2):
                send(part, head, half).start()
    for head in range(KV_HEADS):
        send_fill(head).wait()
        for part in range(PACK_PARTS):
            for half in range(2):
                send(part, head, half).wait()


def pack(block_fill, cache_pool):
    tokens = OWN_BLOCKS * BLK_TOKENS
    return pl.pallas_call(
        pack_kernel,
        out_shape=jax.ShapeDtypeStruct((KV_HEADS, PIECE_ROWS, 2 * HEAD_DIM), jnp.bfloat16),
        in_specs=[
            pl.BlockSpec(memory_space=pltpu.SMEM),
            pl.BlockSpec(memory_space=pltpu.HBM),
        ],
        out_specs=pl.BlockSpec(memory_space=pltpu.HBM),
        scratch_shapes=[
            pltpu.VMEM((tokens, 2 * WIDTH), jnp.bfloat16),
            pltpu.VMEM((FILL_ROWS, 2 * HEAD_DIM), jnp.bfloat16),
            pltpu.SemaphoreType.DMA((PACK_PARTS,)),
            pltpu.SemaphoreType.DMA((PACK_PARTS * KV_HEADS * 2 + KV_HEADS,)),
        ],
        compiler_params=pltpu.CompilerParams(vmem_limit_bytes=60 * 1024 * 1024),
        name="pack",
    )(block_fill, cache_pool.reshape(tokens, 2 * WIDTH))


def attend_kernel(codes, counts, kv, query, barred, out, fills, keys, values, peaks, sums):
    for source in range(HOLDERS):
        base = source * PIECE_ROWS + OWN_BLOCKS * BLK_TOKENS
        packed = kv[pl.ds(base, FILL_ROWS), :].astype(jnp.float32)
        for third in range(OWN_BLOCKS // FILL_ROWS):
            start = third // 2 * HEAD_DIM
            lanes = packed[:, start : start + HEAD_DIM]
            if third % 2:
                lanes = jnp.concatenate([lanes[:, 64:], lanes[:, :64]], axis=1)
            place = pl.ds(source * OWN_BLOCKS + third * FILL_ROWS, FILL_ROWS)
            fills[place, :] = lanes
    values[:, :, HEAD_DIM:] = jnp.ones((TOGETHER, TOKENS, HEAD_DIM), jnp.bfloat16)
    row_rollout = lax.broadcasted_iota(jnp.int32, (ROWS, HEAD_DIM), 0) // GROUP
    lane = lax.broadcasted_iota(jnp.int32, (ROWS, HEAD_DIM), 1)
    member_lanes = jnp.where(row_rollout == lane, 1.0, 0.0).astype(jnp.bfloat16)
    token = lax.broadcasted_iota(jnp.int32, (BLK_TOKENS, HEAD_DIM), 0).astype(jnp.float32)
    pick = lax.broadcasted_iota(jnp.int32, (8, HEAD_DIM), 0)
    pick_lane = lax.broadcasted_iota(jnp.int32, (8, HEAD_DIM), 1)
    picked = jnp.where(pick == pick_lane, 1.0, 0.0).astype(jnp.bfloat16)

    def chunk_scores(tile, chunk, lane_of):
        rows = query[pl.ds(pl.multiple_of(tile * ROWS, ROWS), ROWS), :]
        left = jnp.concatenate([rows, member_lanes], axis=1)
        for slot in range(CHUNK):
            number = chunk * CHUNK + slot
            code = codes[tile * BLOCKS + number]
            source = (code * 1366) >> 16
            row = pl.multiple_of((code + source) * BLK_TOKENS, BLK_TOKENS)
            place = pl.ds(slot * BLK_TOKENS, BLK_TOKENS)
            keys[lane_of, place, 0:HEAD_DIM] = kv[pl.ds(row, BLK_TOKENS), 0:HEAD_DIM]
            values[lane_of, place, 0:HEAD_DIM] = kv[pl.ds(row, BLK_TOKENS), HEAD_DIM:]
            fill = jnp.where(number < counts[tile], fills[pl.ds(code, 1), :], 0.0)
            keys[lane_of, place, HEAD_DIM:] = jnp.where(
                token < fill, barred[pl.ds(tile * BLOCKS + code, 1), :], DEAD
            ).astype(jnp.bfloat16)
        return lax.dot_general(
            left, keys[lane_of], (((1,), (1,)), ((), ())), preferred_element_type=jnp.float32
        )

    def highest(found, low):
        peak = jnp.maximum(jnp.max(found, axis=1, keepdims=True) * SCALE, low)
        return peak.astype(jnp.bfloat16).astype(jnp.float32)

    def summed(found, peak, lane_of):
        weights = jnp.exp(found * SCALE - peak).astype(jnp.bfloat16)
        return jnp.dot(weights, values[lane_of], preferred_element_type=jnp.float32)

    def put_out(tile, peak, sums):
        total = sums[:, HEAD_DIM:]
        coarse = total.astype(jnp.bfloat16).astype(jnp.float32)
        stats = jnp.where(lane == 0, peak, jnp.where(lane == 1, coarse, total - coarse))
        flat = lax.dot_general(
            picked,
            stats.astype(jnp.bfloat16),
            (((1,), (1,)), ((), ())),
            preferred_element_type=jnp.float32,
        )
        for part in range(TILE // 32):
            count = 32 * GROUP
            out[tile * (TILE // 32) + part, 0:count, :] = sums[
                part * count : (part + 1) * count, 0:HEAD_DIM
            ].astype(jnp.bfloat16)
            both = jnp.concatenate(
                [
                    flat[:, part * count : part * count + HEAD_DIM],
                    flat[:, part * count + HEAD_DIM : (part + 1) * count],
                ],
                axis=0,
            )
            out[tile * (TILE // 32) + part, count:, :] = both.astype(jnp.bfloat16)

    def long_tile(tile):
        chunks = (counts[tile] + CHUNK - 1) // CHUNK
        found = chunk_scores(tile, 0, 0)
        peak = highest(found, LOW)
        peaks[...] = jnp.broadcast_to(peak, (ROWS, HEAD_DIM))
        sums[...] = summed(found, peak, 0)

        def more(chunk, _):
            found = chunk_scores(tile, chunk, 0)
            old = peaks[:, 0:1]
            peak = highest(found, old)
            sums[...] = sums[...] * jnp.exp(old - peak) + summed(found, peak, 0)
            peaks[...] = jnp.broadcast_to(peak, (ROWS, HEAD_DIM))
            return 0

        lax.fori_loop(1, chunks, more, 0)
        put_out(tile, peaks[...], sums[...])

    def some_tiles(step, _):
        tiles = [step * TOGETHER + k for k in range(TOGETHER)]
        most = counts[tiles[0]]
        for tile in tiles[1:]:
            most = jnp.maximum(most, counts[tile])

        @pl.when(most <= CHUNK)
        def _():
            found = [chunk_scores(tile, 0, k) for k, tile in enumerate(tiles)]
            peak = [highest(one, LOW) for one in found]
            added = [summed(found[k], peak[k], k) for k in range(TOGETHER)]
            for k, tile in enumerate(tiles):
                put_out(tile, peak[k], added[k])

        @pl.when(most > CHUNK)
        def _():
            lax.fori_loop(0, TOGETHER, lambda k, _: long_tile(tiles[0] + k) or 0, 0)

        return 0

    lax.fori_loop(0, counts.shape[0] // TOGETHER, some_tiles, 0)


def attend(codes, counts, kv, query, barred):
    vmem = pl.BlockSpec(memory_space=pltpu.VMEM)
    smem = pl.BlockSpec(memory_space=pltpu.SMEM)
    sources = query.shape[0] // (32 * GROUP)
    return pl.pallas_call(
        attend_kernel,
        out_shape=jax.ShapeDtypeStruct((sources, OUT_ROWS, HEAD_DIM), jnp.bfloat16),
        in_specs=[smem, smem, vmem, vmem, vmem],
        out_specs=vmem,
        scratch_shapes=[
            pltpu.VMEM((BLOCKS, HEAD_DIM), jnp.float32),
            pltpu.VMEM((TOGETHER, TOKENS, 2 * HEAD_DIM), jnp.bfloat16),
            pltpu.VMEM((TOGETHER, TOKENS, 2 * HEAD_DIM), jnp.bfloat16),
            pltpu.VMEM((ROWS, HEAD_DIM), jnp.float32),
            pltpu.VMEM((ROWS, 2 * HEAD_DIM), jnp.float32),
        ],
        compiler_params=pltpu.CompilerParams(vmem_limit_bytes=50 * 1024 * 1024),
        cost_estimate=pl.CostEstimate(
            flops=4 * 4096 * 512 * 256, bytes_accessed=6 << 20, transcendentals=4096 * 512
        ),
        name="attend",
    )(codes, counts, kv, query, barred)


def finish_kernel(parts, query, entry, out, peaks, totals, ended):
    sources = parts.shape[0]
    count = parts.shape[1] - 16
    which = lax.broadcasted_iota(jnp.int32, (8, 2 * HEAD_DIM), 0)
    lane = lax.broadcasted_iota(jnp.int32, (8, 2 * HEAD_DIM), 1)
    spread = jnp.where(
        lane < HEAD_DIM, jnp.where(which == 0, 1.0, 0.0), jnp.where((which == 1) | (which == 2), 1.0, 0.0)
    ).astype(jnp.bfloat16)
    rollouts = count // GROUP
    own_key = jnp.broadcast_to(
        entry[:, 0:HEAD_DIM].astype(jnp.float32)[:, None, :], (rollouts, GROUP, HEAD_DIM)
    ).reshape(count, HEAD_DIM)
    own_value = jnp.broadcast_to(
        entry[:, HEAD_DIM:].astype(jnp.float32)[:, None, :], (rollouts, GROUP, HEAD_DIM)
    ).reshape(count, HEAD_DIM)
    own = jnp.sum(query[...].astype(jnp.float32) * own_key, axis=1, keepdims=True) * SCALE
    highest = jnp.broadcast_to(own, (count, HEAD_DIM))
    for source in range(sources):
        flat = parts[source, count:, :].astype(jnp.float32)
        for half in range(count // HEAD_DIM):
            wide = lax.dot_general(
                flat[half * 8 : half * 8 + 8, :].astype(jnp.bfloat16),
                spread,
                (((0,), (0,)), ((), ())),
                preferred_element_type=jnp.float32,
            )
            place = pl.ds(half * HEAD_DIM, HEAD_DIM)
            peaks[source, place, :] = wide[:, :HEAD_DIM]
            totals[source, place, :] = wide[:, HEAD_DIM:]
        highest = jnp.maximum(highest, peaks[source])
    weight = jnp.exp(own - highest)
    total = weight
    accum = weight * own_value
    for source in range(sources):
        weight = jnp.exp(peaks[source] - highest)
        total = total + weight * totals[source]
        accum = accum + weight * parts[source, 0:count, :].astype(jnp.float32)
    ended[...] = accum / total
    for head in range(GROUP):
        out[:, head * HEAD_DIM : (head + 1) * HEAD_DIM] = ended[
            pl.ds(head, rollouts, stride=GROUP), :
        ].astype(jnp.bfloat16)


def finish(parts, query, entry):
    count = query.shape[0]
    vmem = pl.BlockSpec(memory_space=pltpu.VMEM)
    return pl.pallas_call(
        finish_kernel,
        out_shape=jax.ShapeDtypeStruct((count // GROUP, WIDTH), jnp.bfloat16),
        in_specs=[vmem, vmem, vmem],
        out_specs=vmem,
        scratch_shapes=[
            pltpu.VMEM((parts.shape[0], count, HEAD_DIM), jnp.float32),
            pltpu.VMEM((parts.shape[0], count, HEAD_DIM), jnp.float32),
            pltpu.VMEM((count, HEAD_DIM), jnp.float32),
        ],
        compiler_params=pltpu.CompilerParams(vmem_limit_bytes=50 * 1024 * 1024),
        name="finish",
    )(parts, query, entry)


def place_kernel(node, *refs):
    pairs, out = refs[:-1], refs[-1]
    chips = len(pairs)
    for hop in range(chips):
        chip = lax.rem(node[0] // 2 - hop + chips, chips)
        for which in range(2):
            core = lax.rem(node[0] + which, 2)
            start = pl.multiple_of((chip * 2 + core) * WIDTH, WIDTH)
            out[:, pl.ds(start, WIDTH)] = pairs[hop][which]


def place_heads(node, pairs):
    vmem = pl.BlockSpec(memory_space=pltpu.VMEM)
    rollouts = pairs[0].shape[1]
    return pl.pallas_call(
        place_kernel,
        out_shape=jax.ShapeDtypeStruct((rollouts, HEADS * HEAD_DIM), jnp.bfloat16),
        in_specs=[pl.BlockSpec(memory_space=pltpu.SMEM)] + [vmem] * len(pairs),
        out_specs=vmem,
        compiler_params=pltpu.CompilerParams(vmem_limit_bytes=16 * 1024 * 1024),
        name="place_heads",
    )(node.reshape(1).astype(jnp.int32), *pairs)


def local_number(ids, column):
    device = ids // OWN_BLOCKS
    here = (device % 16) == column
    return jnp.where(here, (device // 16) * OWN_BLOCKS + ids % OWN_BLOCKS, -1)


def visits(root, lists):
    tiles, _, rollouts = lists.shape
    numbers = jnp.arange(BLOCKS, dtype=jnp.int32)
    everyone = jnp.any(root[:, None] == numbers, axis=0)
    member = jnp.any(lists[:, :, None, :] == numbers[None, None, :, None], axis=1)
    member = member | everyone[None, :, None]
    hit = jnp.any(member, axis=2)
    counts = jnp.sum(hit, axis=1, dtype=jnp.int32)
    before = (numbers[:, None] < numbers[None, :]).astype(jnp.bfloat16)
    place = jnp.dot(hit.astype(jnp.bfloat16), before, preferred_element_type=jnp.float32)
    place = jnp.where(hit, place.astype(jnp.int32), -1)
    codes = jnp.sum(jnp.where(place[:, None, :] == numbers[None, :, None], numbers, 0), axis=2)
    barred = jnp.pad(jnp.where(member, 0.0, DEAD), ((0, 0), (0, 0), (0, HEAD_DIM - rollouts)))
    return (
        codes.astype(jnp.int32).reshape(tiles * BLOCKS),
        counts,
        barred.reshape(tiles * BLOCKS, HEAD_DIM),
    )


def per_device(queries, new_entry, block_lists, list_lengths, block_fill, cache_pool):
    node = lax.axis_index("node")
    column = lax.axis_index("group")
    groups = lax.axis_size("group")
    own_rows = queries.shape[0]

    sent = pack(block_fill, cache_pool)
    kv = lax.all_to_all(sent, "node", split_axis=0, concat_axis=0, tiled=True)
    kv = kv.reshape(HOLDERS * PIECE_ROWS, 2 * HEAD_DIM)

    head_query = lax.dynamic_slice_in_dim(queries, node * WIDTH, WIDTH, axis=1)
    entries = jnp.arange(LIST, dtype=jnp.int32)[None, :]
    tail = jnp.where(entries < list_lengths[:, None], block_lists, 8191)[:, ROOT_BLOCKS:]
    coded = jnp.concatenate([tail // 128, tail % 128], axis=1).astype(jnp.bfloat16)
    coded = jnp.pad(coded, ((0, 0), (0, HEAD_DIM - coded.shape[1])))
    told = jnp.concatenate([head_query, coded], axis=1)
    sent, told = lax.optimization_barrier((sent, told))
    side = 4
    def shifted(value, hop_x, hop_z):
        pairs = [
            (x * side + z, (x + hop_x) % side * side + (z + hop_z) % side)
            for x in range(side)
            for z in range(side)
        ]
        return lax.ppermute(value, "group", pairs)

    line = jnp.stack([told] + [shifted(told, 0, hop) for hop in range(1, side)])
    told = jnp.stack([line] + [shifted(line, hop, 0) for hop in range(1, side)])
    column_x, column_z = column // side, column % side
    order = jnp.arange(side, dtype=jnp.int32)
    told = jnp.take(told, (column_x - order) % side, axis=0)
    told = jnp.take(told, (column_z - order) % side, axis=1)
    told = told.reshape((groups,) + told.shape[2:])
    all_query = told[:, :, :WIDTH].reshape(groups * own_rows * GROUP, HEAD_DIM)
    coded = told[:, :, WIDTH:].astype(jnp.int32).reshape(groups * own_rows, HEAD_DIM)
    count = LIST - ROOT_BLOCKS
    ids = coded[:, :count] * 128 + coded[:, count : 2 * count]
    tail = jnp.where(ids < 8191, local_number(ids, column), -1)
    root = local_number(block_lists[0, :ROOT_BLOCKS], column)
    tiles = groups * own_rows // TILE
    codes, counts, barred = visits(
        root, jnp.transpose(tail.reshape(tiles, TILE, count), (0, 2, 1))
    )
    partial = attend(codes, counts, kv, all_query, barred)
    parts = lax.all_to_all(partial, "group", split_axis=0, concat_axis=0, tiled=True)
    key = lax.dynamic_slice_in_dim(new_entry, node * HEAD_DIM, HEAD_DIM, axis=1)
    value = lax.dynamic_slice_in_dim(new_entry, WIDTH + node * HEAD_DIM, HEAD_DIM, axis=1)
    done = finish(
        parts,
        head_query.reshape(own_rows * GROUP, HEAD_DIM),
        jnp.concatenate([key, value], axis=1),
    )
    nodes = lax.axis_size("node")
    other = lax.ppermute(done, "node", [(i, i ^ 1) for i in range(nodes)])
    pair = jnp.stack([done, other])
    pairs = [pair] + [
        lax.ppermute(pair, "node", [(i, (i + 2 * hop) % nodes) for i in range(nodes)])
        for hop in range(1, nodes // 2)
    ]
    return place_heads(node, pairs)


def solution(mesh):
    return jax.shard_map(
        per_device,
        mesh=mesh,
        in_specs=(
            P("group", None),
            P("group", None),
            P("group", None),
            P("group"),
            P(("node", "group")),
            P(("node", "group"), None, None),
        ),
        out_specs=P("group", None),
        check_vma=False,
    )
```

```python
import functools
import math

import jax
import jax.numpy as jnp
from jax import lax
from jax.experimental import pallas as pl
from jax.experimental.pallas import tpu as pltpu
from jax.sharding import PartitionSpec as P

HEADS = 64
KV_HEADS = 8
HEAD_DIM = 128
BLK_TOKENS = 16
ROOT_BLOCKS = 40
LIST = 64
WIDTH = KV_HEADS * HEAD_DIM
GROUP = HEADS // KV_HEADS
SCALE = 1.0 / math.sqrt(HEAD_DIM)
SCALE2 = SCALE * math.log2(math.e)

HOLDERS = 8
OWN_BLOCKS = 48
BLOCKS = HOLDERS * OWN_BLOCKS
PIECE_ROWS = OWN_BLOCKS * BLK_TOKENS
MARK = 2.0**120
TILE = 64
CHUNK = 40
SIZES = (24, 32, 40)
ROWS = TILE * GROUP
PACK_PARTS = 4
TOGETHER = 4
TOKENS = CHUNK * BLK_TOKENS
OUT_ROWS = 32 * GROUP + 16
LOW = -1e9
DEAD = -1e30


def pack_kernel(fill, pool, out, staged, ready, arrived, left):
    span = PIECE_ROWS // PACK_PARTS

    def fetch(part):
        place = pl.ds(part * span, span)
        return pltpu.make_async_copy(pool.at[place, :], staged.at[part], arrived.at[part])

    def send(part, head):
        return pltpu.make_async_copy(
            ready.at[part, head],
            out.at[head, pl.ds(part * span, span), :],
            left.at[part * KV_HEADS + head],
        )

    for part in range(PACK_PARTS):
        fetch(part).start()
    token = lax.broadcasted_iota(jnp.int32, (BLK_TOKENS, HEAD_DIM), 0)
    blocks = span // BLK_TOKENS
    for part in range(PACK_PARTS):
        fetch(part).wait()
        live = [token < fill[part * blocks + block] for block in range(blocks)]
        for head in range(KV_HEADS):
            lanes = slice(head * HEAD_DIM, (head + 1) * HEAD_DIM)
            for block in range(blocks):
                place = slice(block * BLK_TOKENS, (block + 1) * BLK_TOKENS)
                key = staged[part, place, lanes].astype(jnp.float32)
                ready[part, head, place, 0:HEAD_DIM] = jnp.where(live[block], key, MARK).astype(
                    jnp.bfloat16
                )
            lanes = slice(WIDTH + head * HEAD_DIM, WIDTH + (head + 1) * HEAD_DIM)
            ready[part, head, :, HEAD_DIM:] = staged[part, :, lanes]
            send(part, head).start()
    for part in range(PACK_PARTS):
        for head in range(KV_HEADS):
            send(part, head).wait()


def pack(block_fill, cache_pool):
    span = PIECE_ROWS // PACK_PARTS
    hbm = pl.BlockSpec(memory_space=pltpu.HBM)
    return pl.pallas_call(
        pack_kernel,
        out_shape=jax.ShapeDtypeStruct((KV_HEADS, PIECE_ROWS, 2 * HEAD_DIM), jnp.bfloat16),
        in_specs=[pl.BlockSpec(memory_space=pltpu.SMEM), hbm],
        out_specs=hbm,
        scratch_shapes=[
            pltpu.VMEM((PACK_PARTS, span, 2 * WIDTH), jnp.bfloat16),
            pltpu.VMEM((PACK_PARTS, KV_HEADS, span, 2 * HEAD_DIM), jnp.bfloat16),
            pltpu.SemaphoreType.DMA((PACK_PARTS,)),
            pltpu.SemaphoreType.DMA((PACK_PARTS * KV_HEADS,)),
        ],
        compiler_params=pltpu.CompilerParams(vmem_limit_bytes=60 * 1024 * 1024),
        name="pack",
    )(block_fill, cache_pool.reshape(PIECE_ROWS, 2 * WIDTH))


def attend_kernel(codes, counts, group, kv, query, barred, out, keys, values, peaks, sums):
    values[:, :, HEAD_DIM:] = jnp.ones((TOGETHER, TOKENS, HEAD_DIM), jnp.bfloat16)
    row_rollout = lax.broadcasted_iota(jnp.int32, (ROWS, HEAD_DIM), 0) // GROUP
    lane = lax.broadcasted_iota(jnp.int32, (ROWS, HEAD_DIM), 1)
    member_lanes = jnp.where(row_rollout == lane, 1.0, 0.0).astype(jnp.bfloat16)
    pick = lax.broadcasted_iota(jnp.int32, (8, HEAD_DIM), 0)
    pick_lane = lax.broadcasted_iota(jnp.int32, (8, HEAD_DIM), 1)
    picked = jnp.where(pick == pick_lane, 1.0, 0.0).astype(jnp.bfloat16)

    def chunk_scores(tile, chunk, lane_of, size=CHUNK):
        rows = query[pl.ds(pl.multiple_of(tile * ROWS, ROWS), ROWS), :]
        left = jnp.concatenate([rows, member_lanes], axis=1)
        for slot in range(size):
            number = chunk * CHUNK + slot
            code = codes[tile * BLOCKS + number]
            row = pl.multiple_of(code * BLK_TOKENS, BLK_TOKENS)
            place = pl.ds(slot * BLK_TOKENS, BLK_TOKENS)
            key = kv[pl.ds(row, BLK_TOKENS), 0:HEAD_DIM].astype(jnp.float32)
            live = (key < MARK) & (number < counts[tile])
            keys[lane_of, place, 0:HEAD_DIM] = jnp.where(live, key, 0.0).astype(jnp.bfloat16)
            keys[lane_of, place, HEAD_DIM:] = jnp.where(
                live, barred[pl.ds(tile * BLOCKS + code, 1), :], DEAD
            ).astype(jnp.bfloat16)
            values[lane_of, place, 0:HEAD_DIM] = kv[pl.ds(row, BLK_TOKENS), HEAD_DIM:]
        return lax.dot_general(
            left,
            keys[lane_of, 0 : size * BLK_TOKENS],
            (((1,), (1,)), ((), ())),
            preferred_element_type=jnp.float32,
        )

    def highest(found, low):
        peak = jnp.maximum(jnp.max(found, axis=1, keepdims=True) * SCALE2, low)
        return peak.astype(jnp.bfloat16).astype(jnp.float32)

    def summed(found, peak, lane_of):
        weights = jnp.exp2(found * SCALE2 - peak).astype(jnp.bfloat16)
        return jnp.dot(
            weights, values[lane_of, 0 : found.shape[1]], preferred_element_type=jnp.float32
        )

    def put_out(tile, peak, sums):
        total = sums[:, HEAD_DIM:]
        coarse = total.astype(jnp.bfloat16).astype(jnp.float32)
        stats = jnp.where(lane == 0, peak, jnp.where(lane == 1, coarse, total - coarse))
        flat = lax.dot_general(
            picked,
            stats.astype(jnp.bfloat16),
            (((1,), (1,)), ((), ())),
            preferred_element_type=jnp.float32,
        )
        for part in range(TILE // 32):
            count = 32 * GROUP
            owner = tile * (TILE // 32) + part
            owner = (((group[0] >> 2) - (owner >> 2)) & 3) * 4 + ((group[0] - owner) & 3)
            out[owner, 0:count, :] = sums[
                part * count : (part + 1) * count, 0:HEAD_DIM
            ].astype(jnp.bfloat16)
            both = jnp.concatenate(
                [
                    flat[:, part * count : part * count + HEAD_DIM],
                    flat[:, part * count + HEAD_DIM : (part + 1) * count],
                ],
                axis=0,
            )
            out[owner, count:, :] = both.astype(jnp.bfloat16)

    def long_tile(tile):
        chunks = (counts[tile] + CHUNK - 1) // CHUNK
        found = chunk_scores(tile, 0, 0)
        peak = highest(found, LOW)
        peaks[...] = jnp.broadcast_to(peak, (ROWS, HEAD_DIM))
        sums[...] = summed(found, peak, 0)

        def more(chunk, _):
            found = chunk_scores(tile, chunk, 0)
            old = peaks[:, 0:1]
            peak = highest(found, old)
            sums[...] = sums[...] * jnp.exp2(old - peak) + summed(found, peak, 0)
            peaks[...] = jnp.broadcast_to(peak, (ROWS, HEAD_DIM))
            return 0

        lax.fori_loop(1, chunks, more, 0)
        put_out(tile, peaks[...], sums[...])

    def some_tiles(step, _):
        tiles = [step * TOGETHER + k for k in range(TOGETHER)]
        most = counts[tiles[0]]
        for tile in tiles[1:]:
            most = jnp.maximum(most, counts[tile])

        for fewer, size in zip((-1,) + SIZES, SIZES):

            @pl.when((most > fewer) & (most <= size))
            def _():
                found = [chunk_scores(tile, 0, k, size) for k, tile in enumerate(tiles)]
                peak = [highest(one, LOW) for one in found]
                added = [summed(found[k], peak[k], k) for k in range(TOGETHER)]
                for k, tile in enumerate(tiles):
                    put_out(tile, peak[k], added[k])

        @pl.when(most > CHUNK)
        def _():
            lax.fori_loop(0, TOGETHER, lambda k, _: long_tile(tiles[0] + k) or 0, 0)

        return 0

    lax.fori_loop(0, counts.shape[0] // TOGETHER, some_tiles, 0)


def attend(codes, counts, group, kv, query, barred):
    vmem = pl.BlockSpec(memory_space=pltpu.VMEM)
    smem = pl.BlockSpec(memory_space=pltpu.SMEM)
    sources = query.shape[0] // (32 * GROUP)
    return pl.pallas_call(
        attend_kernel,
        out_shape=jax.ShapeDtypeStruct((sources, OUT_ROWS, HEAD_DIM), jnp.bfloat16),
        in_specs=[smem, smem, smem, vmem, vmem, vmem],
        out_specs=vmem,
        scratch_shapes=[
            pltpu.VMEM((TOGETHER, TOKENS, 2 * HEAD_DIM), jnp.bfloat16),
            pltpu.VMEM((TOGETHER, TOKENS, 2 * HEAD_DIM), jnp.bfloat16),
            pltpu.VMEM((ROWS, HEAD_DIM), jnp.float32),
            pltpu.VMEM((ROWS, 2 * HEAD_DIM), jnp.float32),
        ],
        compiler_params=pltpu.CompilerParams(vmem_limit_bytes=26 * 1024 * 1024),
        cost_estimate=pl.CostEstimate(
            flops=4 * 4096 * 512 * 256, bytes_accessed=6 << 20, transcendentals=4096 * 512
        ),
        name="attend",
    )(codes, counts, group, kv, query, barred)


def finish_kernel(parts, query, entry, out, peaks, totals, ended):
    sources = parts.shape[0]
    count = parts.shape[1] - 16
    which = lax.broadcasted_iota(jnp.int32, (8, 2 * HEAD_DIM), 0)
    lane = lax.broadcasted_iota(jnp.int32, (8, 2 * HEAD_DIM), 1)
    spread = jnp.where(
        lane < HEAD_DIM, jnp.where(which == 0, 1.0, 0.0), jnp.where((which == 1) | (which == 2), 1.0, 0.0)
    ).astype(jnp.bfloat16)
    rollouts = count // GROUP
    own_key = jnp.broadcast_to(
        entry[:, 0:HEAD_DIM].astype(jnp.float32)[:, None, :], (rollouts, GROUP, HEAD_DIM)
    ).reshape(count, HEAD_DIM)
    own_value = jnp.broadcast_to(
        entry[:, HEAD_DIM:].astype(jnp.float32)[:, None, :], (rollouts, GROUP, HEAD_DIM)
    ).reshape(count, HEAD_DIM)
    own = jnp.sum(query[...].astype(jnp.float32) * own_key, axis=1, keepdims=True) * SCALE2
    highest = jnp.broadcast_to(own, (count, HEAD_DIM))
    for source in range(sources):
        flat = parts[source, count:, :].astype(jnp.float32)
        for half in range(count // HEAD_DIM):
            wide = lax.dot_general(
                flat[half * 8 : half * 8 + 8, :].astype(jnp.bfloat16),
                spread,
                (((0,), (0,)), ((), ())),
                preferred_element_type=jnp.float32,
            )
            place = pl.ds(half * HEAD_DIM, HEAD_DIM)
            peaks[source, place, :] = wide[:, :HEAD_DIM]
            totals[source, place, :] = wide[:, HEAD_DIM:]
        highest = jnp.maximum(highest, peaks[source])
    weight = jnp.exp2(own - highest)
    total = weight
    accum = weight * own_value
    for source in range(sources):
        weight = jnp.exp2(peaks[source] - highest)
        total = total + weight * totals[source]
        accum = accum + weight * parts[source, 0:count, :].astype(jnp.float32)
    ended[...] = accum / total
    for head in range(GROUP):
        out[:, head * HEAD_DIM : (head + 1) * HEAD_DIM] = ended[
            pl.ds(head, rollouts, stride=GROUP), :
        ].astype(jnp.bfloat16)


def finish(parts, query, entry):
    count = query.shape[0]
    vmem = pl.BlockSpec(memory_space=pltpu.VMEM)
    return pl.pallas_call(
        finish_kernel,
        out_shape=jax.ShapeDtypeStruct((count // GROUP, WIDTH), jnp.bfloat16),
        in_specs=[vmem, vmem, vmem],
        out_specs=vmem,
        scratch_shapes=[
            pltpu.VMEM((parts.shape[0], count, HEAD_DIM), jnp.float32),
            pltpu.VMEM((parts.shape[0], count, HEAD_DIM), jnp.float32),
            pltpu.VMEM((count, HEAD_DIM), jnp.float32),
        ],
        compiler_params=pltpu.CompilerParams(vmem_limit_bytes=50 * 1024 * 1024),
        name="finish",
    )(parts, query, entry)


def place_kernel(node, *refs):
    heads, out = refs[:-1], refs[-1]
    chips = len(heads) // 2
    for which in range(2):
        core = lax.rem(node[0] + which, 2)
        for hop, ref in zip((0, 1, 3, 2), heads[which * chips : (which + 1) * chips]):
            chip = lax.rem(node[0] // 2 - hop + chips, chips)
            start = pl.multiple_of((chip * 2 + core) * WIDTH, WIDTH)
            out[:, pl.ds(start, WIDTH)] = ref[...]


def place_heads(node, mine, other):
    vmem = pl.BlockSpec(memory_space=pltpu.VMEM)
    rollouts = mine[0].shape[0]
    return pl.pallas_call(
        place_kernel,
        out_shape=jax.ShapeDtypeStruct((rollouts, HEADS * HEAD_DIM), jnp.bfloat16),
        in_specs=[pl.BlockSpec(memory_space=pltpu.SMEM)] + [vmem] * (2 * len(mine)),
        out_specs=vmem,
        compiler_params=pltpu.CompilerParams(vmem_limit_bytes=16 * 1024 * 1024),
        name="place_heads",
    )(node.reshape(1).astype(jnp.int32), *mine, *other)


def local_number(ids, column):
    device = ids // OWN_BLOCKS
    here = (device % 16) == column
    return jnp.where(here, (device // 16) * OWN_BLOCKS + ids % OWN_BLOCKS, -1)


def visits(root, lists):
    tiles, _, rollouts = lists.shape
    numbers = jnp.arange(BLOCKS, dtype=jnp.int32)
    everyone = jnp.any(root[:, None] == numbers, axis=0)
    member = jnp.any(lists[:, :, None, :] == numbers[None, None, :, None], axis=1)
    member = member | everyone[None, :, None]
    hit = jnp.any(member, axis=2)
    counts = jnp.sum(hit, axis=1, dtype=jnp.int32)
    before = (numbers[:, None] < numbers[None, :]).astype(jnp.bfloat16)
    place = jnp.dot(hit.astype(jnp.bfloat16), before, preferred_element_type=jnp.float32)
    place = jnp.where(hit, place.astype(jnp.int32), -1)
    codes = jnp.sum(jnp.where(place[:, None, :] == numbers[None, :, None], numbers, 0), axis=2)
    barred = jnp.pad(jnp.where(member, 0.0, DEAD), ((0, 0), (0, 0), (0, HEAD_DIM - rollouts)))
    return (
        codes.astype(jnp.int32).reshape(tiles * BLOCKS),
        counts,
        barred.reshape(tiles * BLOCKS, HEAD_DIM),
    )


def per_device(queries, new_entry, block_lists, list_lengths, block_fill, cache_pool):
    node = lax.axis_index("node")
    column = lax.axis_index("group")
    groups = lax.axis_size("group")
    own_rows = queries.shape[0]

    sent = pack(block_fill, cache_pool)
    kv = lax.all_to_all(sent, "node", split_axis=0, concat_axis=0, tiled=True)
    kv = kv.reshape(HOLDERS * PIECE_ROWS, 2 * HEAD_DIM)

    head_query = lax.dynamic_slice_in_dim(queries, node * WIDTH, WIDTH, axis=1)
    entries = jnp.arange(LIST, dtype=jnp.int32)[None, :]
    tail = jnp.where(entries < list_lengths[:, None], block_lists, 8191)[:, ROOT_BLOCKS:]
    coded = jnp.concatenate([tail // 128, tail % 128], axis=1).astype(jnp.bfloat16)
    coded = jnp.pad(coded, ((0, 0), (0, HEAD_DIM - coded.shape[1])))
    told = jnp.concatenate([head_query, coded], axis=1)
    sent, told = lax.optimization_barrier((sent, told))
    side = 4
    def shifted(value, hop_x, hop_z):
        pairs = [
            (x * side + z, (x + hop_x) % side * side + (z + hop_z) % side)
            for x in range(side)
            for z in range(side)
        ]
        return lax.ppermute(value, "group", pairs)

    line = jnp.stack([told] + [shifted(told, 0, hop) for hop in range(1, side)])
    told = jnp.stack([line] + [shifted(line, hop, 0) for hop in range(1, side)])
    told = told.reshape((groups,) + told.shape[2:])
    all_query = told[:, :, :WIDTH].reshape(groups * own_rows * GROUP, HEAD_DIM)
    coded = told[:, :, WIDTH:].astype(jnp.int32).reshape(groups * own_rows, HEAD_DIM)
    count = LIST - ROOT_BLOCKS
    ids = coded[:, :count] * 128 + coded[:, count : 2 * count]
    tail = jnp.where(ids < 8191, local_number(ids, column), -1)
    root = local_number(block_lists[0, :ROOT_BLOCKS], column)
    tiles = groups * own_rows // TILE
    codes, counts, barred = visits(
        root, jnp.transpose(tail.reshape(tiles, TILE, count), (0, 2, 1))
    )
    group = column.reshape(1).astype(jnp.int32)
    partial = attend(codes, counts, group, kv, all_query, barred)
    parts = lax.all_to_all(partial, "group", split_axis=0, concat_axis=0, tiled=True)
    key = lax.dynamic_slice_in_dim(new_entry, node * HEAD_DIM, HEAD_DIM, axis=1)
    value = lax.dynamic_slice_in_dim(new_entry, WIDTH + node * HEAD_DIM, HEAD_DIM, axis=1)
    done = finish(
        parts,
        head_query.reshape(own_rows * GROUP, HEAD_DIM),
        jnp.concatenate([key, value], axis=1),
    )
    nodes = lax.axis_size("node")

    def from_node(value, to):
        return lax.ppermute(value, "node", [(i, to(i)) for i in range(nodes)])

    def along(hop):
        return lambda i: (i + 2 * hop) % nodes

    mine = [done] + [from_node(done, along(hop)) for hop in (1, 3, 2)]
    other = [from_node(value, lambda i: i ^ 1) for value in mine]
    return place_heads(node, mine, other)


def solution(mesh):
    return jax.shard_map(
        per_device,
        mesh=mesh,
        in_specs=(
            P("group", None),
            P("group", None),
            P("group", None),
            P("group"),
            P(("node", "group")),
            P(("node", "group"), None, None),
        ),
        out_specs=P("group", None),
        check_vma=False,
    )
```

```python
import functools
import math

import jax
import jax.numpy as jnp
from jax import lax
from jax.experimental import pallas as pl
from jax.experimental.pallas import tpu as pltpu
from jax.sharding import PartitionSpec as P

HEADS = 64
KV_HEADS = 8
HEAD_DIM = 128
BLK_TOKENS = 16
ROOT_BLOCKS = 40
LIST = 64
WIDTH = KV_HEADS * HEAD_DIM
GROUP = HEADS // KV_HEADS
SCALE = 1.0 / math.sqrt(HEAD_DIM)
SCALE2 = SCALE * math.log2(math.e)

HOLDERS = 8
OWN_BLOCKS = 48
BLOCKS = HOLDERS * OWN_BLOCKS
PIECE_ROWS = OWN_BLOCKS * BLK_TOKENS
MARK = 2.0**120
TILE = 64
CHUNK = 40
SIZES = (24, 32, 40)
ROWS = TILE * GROUP
PACK_PARTS = 4
TOGETHER = 4
TOKENS = CHUNK * BLK_TOKENS
OUT_ROWS = 32 * GROUP + 16
LOW = -1e9
DEAD = -1e30
NOBODY = 255


def pack_kernel(fill, pool, out, staged, ready, arrived, left):
    span = PIECE_ROWS // PACK_PARTS

    def fetch(part):
        place = pl.ds(part * span, span)
        return pltpu.make_async_copy(pool.at[place, :], staged.at[part], arrived.at[part])

    def send(part, head):
        return pltpu.make_async_copy(
            ready.at[part, head],
            out.at[head, pl.ds(part * span, span), :],
            left.at[part * KV_HEADS + head],
        )

    for part in range(PACK_PARTS):
        fetch(part).start()
    token = lax.broadcasted_iota(jnp.int32, (BLK_TOKENS, HEAD_DIM), 0)
    blocks = span // BLK_TOKENS
    for part in range(PACK_PARTS):
        fetch(part).wait()
        live = [token < fill[part * blocks + block] for block in range(blocks)]
        for head in range(KV_HEADS):
            lanes = slice(head * HEAD_DIM, (head + 1) * HEAD_DIM)
            for block in range(blocks):
                place = slice(block * BLK_TOKENS, (block + 1) * BLK_TOKENS)
                key = staged[part, place, lanes].astype(jnp.float32)
                ready[part, head, place, 0:HEAD_DIM] = jnp.where(live[block], key, MARK).astype(
                    jnp.bfloat16
                )
            lanes = slice(WIDTH + head * HEAD_DIM, WIDTH + (head + 1) * HEAD_DIM)
            ready[part, head, :, HEAD_DIM:] = staged[part, :, lanes]
            send(part, head).start()
    for part in range(PACK_PARTS):
        for head in range(KV_HEADS):
            send(part, head).wait()


def pack(block_fill, cache_pool):
    span = PIECE_ROWS // PACK_PARTS
    hbm = pl.BlockSpec(memory_space=pltpu.HBM)
    return pl.pallas_call(
        pack_kernel,
        out_shape=jax.ShapeDtypeStruct((KV_HEADS, PIECE_ROWS, 2 * HEAD_DIM), jnp.bfloat16),
        in_specs=[pl.BlockSpec(memory_space=pltpu.SMEM), hbm],
        out_specs=hbm,
        scratch_shapes=[
            pltpu.VMEM((PACK_PARTS, span, 2 * WIDTH), jnp.bfloat16),
            pltpu.VMEM((PACK_PARTS, KV_HEADS, span, 2 * HEAD_DIM), jnp.bfloat16),
            pltpu.SemaphoreType.DMA((PACK_PARTS,)),
            pltpu.SemaphoreType.DMA((PACK_PARTS * KV_HEADS,)),
        ],
        compiler_params=pltpu.CompilerParams(vmem_limit_bytes=60 * 1024 * 1024),
        name="pack",
    )(block_fill, cache_pool.reshape(PIECE_ROWS, 2 * WIDTH))


def attend_kernel(codes, counts, group, kv, query, barred, out, keys, values, peaks, sums):
    values[:, :, HEAD_DIM:] = jnp.ones((TOGETHER, TOKENS, HEAD_DIM), jnp.bfloat16)
    row_rollout = lax.broadcasted_iota(jnp.int32, (ROWS, HEAD_DIM), 0) // GROUP
    lane = lax.broadcasted_iota(jnp.int32, (ROWS, HEAD_DIM), 1)

    def member_lanes(parity):
        mine = row_rollout + TILE * parity == lane
        return jnp.where(mine, 1.0, 0.0).astype(jnp.bfloat16)

    members = [member_lanes(parity) for parity in range(2)]
    pick = lax.broadcasted_iota(jnp.int32, (8, HEAD_DIM), 0)
    pick_lane = lax.broadcasted_iota(jnp.int32, (8, HEAD_DIM), 1)
    picked = jnp.where(pick == pick_lane, 1.0, 0.0).astype(jnp.bfloat16)

    def chunk_scores(tile, chunk, lane_of, size=CHUNK, member=None):
        member = member_lanes(tile & 1) if member is None else member
        rows = query[pl.ds(pl.multiple_of(tile * ROWS, ROWS), ROWS), :]
        left = jnp.concatenate([rows, member], axis=1)
        for slot in range(size):
            number = chunk * CHUNK + slot
            code = codes[tile, number]
            row = pl.multiple_of(code * BLK_TOKENS, BLK_TOKENS)
            place = pl.ds(slot * BLK_TOKENS, BLK_TOKENS)
            key = kv[pl.ds(row, BLK_TOKENS), 0:HEAD_DIM].astype(jnp.float32)
            live = (key < MARK) & (number < counts[0, tile])
            keys[lane_of, place, 0:HEAD_DIM] = jnp.where(live, key, 0.0).astype(jnp.bfloat16)
            keys[lane_of, place, HEAD_DIM:] = jnp.where(
                live, barred[pl.ds((tile >> 1) * BLOCKS + code, 1), :], DEAD
            ).astype(jnp.bfloat16)
            values[lane_of, place, 0:HEAD_DIM] = kv[pl.ds(row, BLK_TOKENS), HEAD_DIM:]
        return lax.dot_general(
            left,
            keys[lane_of, 0 : size * BLK_TOKENS],
            (((1,), (1,)), ((), ())),
            preferred_element_type=jnp.float32,
        )

    def highest(found, low):
        peak = jnp.maximum(jnp.max(found, axis=1, keepdims=True) * SCALE2, low)
        return peak.astype(jnp.bfloat16).astype(jnp.float32)

    def summed(found, peak, lane_of):
        weights = jnp.exp2(found * SCALE2 - peak).astype(jnp.bfloat16)
        return jnp.dot(
            weights, values[lane_of, 0 : found.shape[1]], preferred_element_type=jnp.float32
        )

    def put_out(tile, peak, sums):
        total = sums[:, HEAD_DIM:]
        coarse = total.astype(jnp.bfloat16).astype(jnp.float32)
        stats = jnp.where(lane == 0, peak, jnp.where(lane == 1, coarse, total - coarse))
        flat = lax.dot_general(
            picked,
            stats.astype(jnp.bfloat16),
            (((1,), (1,)), ((), ())),
            preferred_element_type=jnp.float32,
        )
        for part in range(TILE // 32):
            count = 32 * GROUP
            owner = tile * (TILE // 32) + part
            owner = (((group[0] >> 2) - (owner >> 2)) & 3) * 4 + ((group[0] - owner) & 3)
            out[owner, 0:count, :] = sums[
                part * count : (part + 1) * count, 0:HEAD_DIM
            ].astype(jnp.bfloat16)
            both = jnp.concatenate(
                [
                    flat[:, part * count : part * count + HEAD_DIM],
                    flat[:, part * count + HEAD_DIM : (part + 1) * count],
                ],
                axis=0,
            )
            out[owner, count:, :] = both.astype(jnp.bfloat16)

    def long_tile(tile):
        chunks = (counts[0, tile] + CHUNK - 1) // CHUNK
        found = chunk_scores(tile, 0, 0)
        peak = highest(found, LOW)
        peaks[...] = jnp.broadcast_to(peak, (ROWS, HEAD_DIM))
        sums[...] = summed(found, peak, 0)

        def more(chunk, _):
            found = chunk_scores(tile, chunk, 0)
            old = peaks[:, 0:1]
            peak = highest(found, old)
            sums[...] = sums[...] * jnp.exp2(old - peak) + summed(found, peak, 0)
            peaks[...] = jnp.broadcast_to(peak, (ROWS, HEAD_DIM))
            return 0

        lax.fori_loop(1, chunks, more, 0)
        put_out(tile, peaks[...], sums[...])

    def some_tiles(step, _):
        tiles = [step * TOGETHER + k for k in range(TOGETHER)]
        most = counts[0, tiles[0]]
        for tile in tiles[1:]:
            most = jnp.maximum(most, counts[0, tile])

        for fewer, size in zip((-1,) + SIZES, SIZES):

            @pl.when((most > fewer) & (most <= size))
            def _():
                found = [
                    chunk_scores(tile, 0, k, size, members[k % 2]) for k, tile in enumerate(tiles)
                ]
                peak = [highest(one, LOW) for one in found]
                added = [summed(found[k], peak[k], k) for k in range(TOGETHER)]
                for k, tile in enumerate(tiles):
                    put_out(tile, peak[k], added[k])

        @pl.when(most > CHUNK)
        def _():
            lax.fori_loop(0, TOGETHER, lambda k, _: long_tile(tiles[0] + k) or 0, 0)

        return 0

    lax.fori_loop(0, codes.shape[0] // TOGETHER, some_tiles, 0)


def attend(codes, counts, group, kv, query, barred):
    vmem = pl.BlockSpec(memory_space=pltpu.VMEM)
    smem = pl.BlockSpec(memory_space=pltpu.SMEM)
    sources = query.shape[0] // (32 * GROUP)
    return pl.pallas_call(
        attend_kernel,
        out_shape=jax.ShapeDtypeStruct((sources, OUT_ROWS, HEAD_DIM), jnp.bfloat16),
        in_specs=[smem, smem, smem, vmem, vmem, vmem],
        out_specs=vmem,
        scratch_shapes=[
            pltpu.VMEM((TOGETHER, TOKENS, 2 * HEAD_DIM), jnp.bfloat16),
            pltpu.VMEM((TOGETHER, TOKENS, 2 * HEAD_DIM), jnp.bfloat16),
            pltpu.VMEM((ROWS, HEAD_DIM), jnp.float32),
            pltpu.VMEM((ROWS, 2 * HEAD_DIM), jnp.float32),
        ],
        compiler_params=pltpu.CompilerParams(vmem_limit_bytes=26 * 1024 * 1024),
        cost_estimate=pl.CostEstimate(
            flops=4 * 4096 * 512 * 256, bytes_accessed=6 << 20, transcendentals=4096 * 512
        ),
        name="attend",
    )(codes, counts, group, kv, query, barred)


def finish_kernel(parts, query, entry, out, peaks, totals, ended):
    sources = parts.shape[0]
    count = parts.shape[1] - 16
    which = lax.broadcasted_iota(jnp.int32, (8, 2 * HEAD_DIM), 0)
    lane = lax.broadcasted_iota(jnp.int32, (8, 2 * HEAD_DIM), 1)
    spread = jnp.where(
        lane < HEAD_DIM, jnp.where(which == 0, 1.0, 0.0), jnp.where((which == 1) | (which == 2), 1.0, 0.0)
    ).astype(jnp.bfloat16)
    rollouts = count // GROUP
    own_key = jnp.broadcast_to(
        entry[:, 0:HEAD_DIM].astype(jnp.float32)[:, None, :], (rollouts, GROUP, HEAD_DIM)
    ).reshape(count, HEAD_DIM)
    own_value = jnp.broadcast_to(
        entry[:, HEAD_DIM:].astype(jnp.float32)[:, None, :], (rollouts, GROUP, HEAD_DIM)
    ).reshape(count, HEAD_DIM)
    own = jnp.sum(query[...].astype(jnp.float32) * own_key, axis=1, keepdims=True) * SCALE2
    highest = jnp.broadcast_to(own, (count, HEAD_DIM))
    for source in range(sources):
        flat = parts[source, count:, :].astype(jnp.float32)
        for half in range(count // HEAD_DIM):
            wide = lax.dot_general(
                flat[half * 8 : half * 8 + 8, :].astype(jnp.bfloat16),
                spread,
                (((0,), (0,)), ((), ())),
                preferred_element_type=jnp.float32,
            )
            place = pl.ds(half * HEAD_DIM, HEAD_DIM)
            peaks[source, place, :] = wide[:, :HEAD_DIM]
            totals[source, place, :] = wide[:, HEAD_DIM:]
        highest = jnp.maximum(highest, peaks[source])
    weight = jnp.exp2(own - highest)
    total = weight
    accum = weight * own_value
    for source in range(sources):
        weight = jnp.exp2(peaks[source] - highest)
        total = total + weight * totals[source]
        accum = accum + weight * parts[source, 0:count, :].astype(jnp.float32)
    ended[...] = accum / total
    for head in range(GROUP):
        out[:, head * HEAD_DIM : (head + 1) * HEAD_DIM] = ended[
            pl.ds(head, rollouts, stride=GROUP), :
        ].astype(jnp.bfloat16)


def finish(parts, query, entry):
    count = query.shape[0]
    vmem = pl.BlockSpec(memory_space=pltpu.VMEM)
    return pl.pallas_call(
        finish_kernel,
        out_shape=jax.ShapeDtypeStruct((count // GROUP, WIDTH), jnp.bfloat16),
        in_specs=[vmem, vmem, vmem],
        out_specs=vmem,
        scratch_shapes=[
            pltpu.VMEM((parts.shape[0], count, HEAD_DIM), jnp.float32),
            pltpu.VMEM((parts.shape[0], count, HEAD_DIM), jnp.float32),
            pltpu.VMEM((count, HEAD_DIM), jnp.float32),
        ],
        compiler_params=pltpu.CompilerParams(vmem_limit_bytes=50 * 1024 * 1024),
        name="finish",
    )(parts, query, entry)


def place_kernel(node, *refs):
    heads, out = refs[:-1], refs[-1]
    chips = len(heads) // 2
    for which in range(2):
        core = lax.rem(node[0] + which, 2)
        for hop, ref in zip((0, 1, 3, 2), heads[which * chips : (which + 1) * chips]):
            chip = lax.rem(node[0] // 2 - hop + chips, chips)
            start = pl.multiple_of((chip * 2 + core) * WIDTH, WIDTH)
            out[:, pl.ds(start, WIDTH)] = ref[...]


def place_heads(node, mine, other):
    vmem = pl.BlockSpec(memory_space=pltpu.VMEM)
    rollouts = mine[0].shape[0]
    return pl.pallas_call(
        place_kernel,
        out_shape=jax.ShapeDtypeStruct((rollouts, HEADS * HEAD_DIM), jnp.bfloat16),
        in_specs=[pl.BlockSpec(memory_space=pltpu.SMEM)] + [vmem] * (2 * len(mine)),
        out_specs=vmem,
        compiler_params=pltpu.CompilerParams(vmem_limit_bytes=16 * 1024 * 1024),
        name="place_heads",
    )(node.reshape(1).astype(jnp.int32), *mine, *other)


def visits_kernel(column, told, root, codes, counts, barred, hits, places):
    entries = LIST - ROOT_BLOCKS
    entry = lax.broadcasted_iota(jnp.int32, (2 * entries, HEAD_DIM), 0)
    lane = lax.broadcasted_iota(jnp.int32, (2 * entries, HEAD_DIM), 1)
    picked = jnp.where(entry == lane, 1.0, 0.0).astype(jnp.bfloat16)
    dims = (((1,), (1,)), ((), ()))
    turned = lax.dot_general(picked, told[...], dims, preferred_element_type=jnp.float32)
    turned = turned.astype(jnp.int32)

    def local(device, place):
        here = ((device & 15) == column[0]) & (device < NOBODY)
        return jnp.where(here, (device >> 4) * OWN_BLOCKS + place, -1)

    listed = local(turned[0:entries], turned[entries:])
    root_row = local(root[0:1, :], root[1:2, :])
    span = 64
    for part in range(BLOCKS // span):
        rows = slice(part * span, (part + 1) * span)
        number = lax.broadcasted_iota(jnp.int32, (span, HEAD_DIM), 0) + part * span
        lane = lax.broadcasted_iota(jnp.int32, (span, HEAD_DIM), 1)
        everyone = jnp.max(jnp.where(root_row == number, 1.0, 0.0), axis=1, keepdims=True)
        found = jnp.zeros((span, HEAD_DIM), jnp.float32)
        for pair in range(told.shape[0] // HEAD_DIM):
            member = jnp.broadcast_to(everyone, (span, HEAD_DIM))
            for index in range(entries):
                row = listed[index : index + 1, pair * HEAD_DIM : (pair + 1) * HEAD_DIM]
                member = jnp.where(row == number, 1.0, member)
            barred[pl.ds(pair * BLOCKS + part * span, span), :] = jnp.where(
                member > 0.5, 0.0, DEAD
            )
            for parity in range(2):
                mine = (lane < TILE) if parity == 0 else (lane >= TILE)
                hit = jnp.max(jnp.where(mine, member, 0.0), axis=1, keepdims=True)
                found = jnp.where(lane == 2 * pair + parity, hit, found)
        hits[rows, :] = found
    hit = hits[...]
    counts[...] = jnp.broadcast_to(jnp.sum(hit, axis=0, keepdims=True), counts.shape).astype(
        jnp.int32
    )
    row = lax.broadcasted_iota(jnp.int32, (BLOCKS, BLOCKS), 0)
    col = lax.broadcasted_iota(jnp.int32, (BLOCKS, BLOCKS), 1)
    before = jnp.where(col < row, 1.0, 0.0).astype(jnp.bfloat16)
    place = jnp.dot(before, hit.astype(jnp.bfloat16), preferred_element_type=jnp.float32)
    places[...] = jnp.where(hit > 0.5, place, -1.0)
    most = jnp.max(jnp.sum(hit, axis=0, keepdims=True))

    def listing(width):
        wide = lax.broadcasted_iota(jnp.int32, (BLOCKS, width), 1).astype(jnp.float32)
        number = lax.broadcasted_iota(jnp.int32, (BLOCKS, width), 0)
        for tile in range(codes.shape[0]):
            there = places[:, tile : tile + 1] == wide
            found = jnp.sum(jnp.where(there, number, 0), axis=0, keepdims=True)
            codes[tile : tile + 1, 0:width] = found

    @pl.when(most <= HEAD_DIM)
    def _():
        listing(HEAD_DIM)
        codes[:, HEAD_DIM:] = jnp.zeros((codes.shape[0], BLOCKS - HEAD_DIM), jnp.int32)

    @pl.when(most > HEAD_DIM)
    def _():
        listing(BLOCKS)


def visits(column, told, root):
    tiles = told.shape[0] // TILE
    vmem = pl.BlockSpec(memory_space=pltpu.VMEM)
    return pl.pallas_call(
        visits_kernel,
        out_shape=[
            jax.ShapeDtypeStruct((tiles, BLOCKS), jnp.int32),
            jax.ShapeDtypeStruct((8, HEAD_DIM), jnp.int32),
            jax.ShapeDtypeStruct((tiles // 2 * BLOCKS, HEAD_DIM), jnp.float32),
        ],
        in_specs=[pl.BlockSpec(memory_space=pltpu.SMEM), vmem, vmem],
        out_specs=[vmem] * 3,
        scratch_shapes=[
            pltpu.VMEM((BLOCKS, HEAD_DIM), jnp.float32),
            pltpu.VMEM((BLOCKS, HEAD_DIM), jnp.float32),
        ],
        compiler_params=pltpu.CompilerParams(vmem_limit_bytes=26 * 1024 * 1024),
        cost_estimate=pl.CostEstimate(flops=10**8, bytes_accessed=2 << 20, transcendentals=0),
        name="visits",
    )(column, told, root)


def per_device(queries, new_entry, block_lists, list_lengths, block_fill, cache_pool):
    node = lax.axis_index("node")
    column = lax.axis_index("group")
    groups = lax.axis_size("group")
    own_rows = queries.shape[0]

    sent = pack(block_fill, cache_pool)
    kv = lax.all_to_all(sent, "node", split_axis=0, concat_axis=0, tiled=True)
    kv = kv.reshape(HOLDERS * PIECE_ROWS, 2 * HEAD_DIM)

    head_query = lax.dynamic_slice_in_dim(queries, node * WIDTH, WIDTH, axis=1)
    entries = jnp.arange(LIST, dtype=jnp.int32)[None, :]
    listed = entries < list_lengths[:, None]
    device = jnp.where(listed, block_lists // OWN_BLOCKS, NOBODY)[:, ROOT_BLOCKS:]
    place = (block_lists % OWN_BLOCKS)[:, ROOT_BLOCKS:]
    coded = jnp.concatenate([device, place], axis=1).astype(jnp.bfloat16)
    coded = jnp.pad(coded, ((0, 0), (0, HEAD_DIM - coded.shape[1])))
    told = jnp.concatenate([head_query, coded], axis=1)
    sent, told = lax.optimization_barrier((sent, told))
    side = 4
    def shifted(value, hop_x, hop_z):
        pairs = [
            (x * side + z, (x + hop_x) % side * side + (z + hop_z) % side)
            for x in range(side)
            for z in range(side)
        ]
        return lax.ppermute(value, "group", pairs)

    line = jnp.stack([told] + [shifted(told, 0, hop) for hop in range(1, side)])
    told = jnp.stack([line] + [shifted(line, hop, 0) for hop in range(1, side)])
    told = told.reshape((groups,) + told.shape[2:])
    all_query = told[:, :, :WIDTH].reshape(groups * own_rows * GROUP, HEAD_DIM)
    coded = told[:, :, WIDTH:].reshape(groups * own_rows, HEAD_DIM)
    root = block_lists[0, :ROOT_BLOCKS]
    root = jnp.stack([root // OWN_BLOCKS, root % OWN_BLOCKS])
    root = jnp.pad(root, ((0, 6), (0, HEAD_DIM - ROOT_BLOCKS)), constant_values=NOBODY)
    group = column.reshape(1).astype(jnp.int32)
    codes, counts, barred = visits(group, coded, root)
    partial = attend(codes, counts, group, kv, all_query, barred)
    parts = lax.all_to_all(partial, "group", split_axis=0, concat_axis=0, tiled=True)
    key = lax.dynamic_slice_in_dim(new_entry, node * HEAD_DIM, HEAD_DIM, axis=1)
    value = lax.dynamic_slice_in_dim(new_entry, WIDTH + node * HEAD_DIM, HEAD_DIM, axis=1)
    done = finish(
        parts,
        head_query.reshape(own_rows * GROUP, HEAD_DIM),
        jnp.concatenate([key, value], axis=1),
    )
    nodes = lax.axis_size("node")

    def from_node(value, to):
        return lax.ppermute(value, "node", [(i, to(i)) for i in range(nodes)])

    def along(hop):
        return lambda i: (i + 2 * hop) % nodes

    mine = [done] + [from_node(done, along(hop)) for hop in (1, 3, 2)]
    other = [from_node(value, lambda i: i ^ 1) for value in mine]
    return place_heads(node, mine, other)


def solution(mesh):
    return jax.shard_map(
        per_device,
        mesh=mesh,
        in_specs=(
            P("group", None),
            P("group", None),
            P("group", None),
            P("group"),
            P(("node", "group")),
            P(("node", "group"), None, None),
        ),
        out_specs=P("group", None),
        check_vma=False,
    )
```

```python
import functools
import math

import jax
import jax.numpy as jnp
from jax import lax
from jax.experimental import pallas as pl
from jax.experimental.pallas import tpu as pltpu
from jax.sharding import PartitionSpec as P

HEADS = 64
KV_HEADS = 8
HEAD_DIM = 128
BLK_TOKENS = 16
ROOT_BLOCKS = 40
LIST = 64
WIDTH = KV_HEADS * HEAD_DIM
GROUP = HEADS // KV_HEADS
SCALE = 1.0 / math.sqrt(HEAD_DIM)
SCALE2 = SCALE * math.log2(math.e)

HOLDERS = 8
OWN_BLOCKS = 48
BLOCKS = HOLDERS * OWN_BLOCKS
PIECE_ROWS = OWN_BLOCKS * BLK_TOKENS
MARK = 2.0**120
TILE = 64
CHUNK = 40
SIZES = (24, 32, 40)
ROWS = TILE * GROUP
PACK_PARTS = 4
TOGETHER = 4
TOKENS = CHUNK * BLK_TOKENS
OUT_ROWS = 32 * GROUP + 16
LOW = -1e9
DEAD = -1e30
NOBODY = 255


def pack_kernel(fill, pool, out, staged, ready, arrived, left):
    span = PIECE_ROWS // PACK_PARTS

    def fetch(part):
        place = pl.ds(part * span, span)
        return pltpu.make_async_copy(pool.at[place, :], staged.at[part], arrived.at[part])

    def send(part, head):
        return pltpu.make_async_copy(
            ready.at[part, head],
            out.at[head, pl.ds(part * span, span), :],
            left.at[part * KV_HEADS + head],
        )

    for part in range(PACK_PARTS):
        fetch(part).start()
    token = lax.broadcasted_iota(jnp.int32, (BLK_TOKENS, HEAD_DIM), 0)
    blocks = span // BLK_TOKENS
    for part in range(PACK_PARTS):
        fetch(part).wait()
        live = [token < fill[part * blocks + block] for block in range(blocks)]
        for head in range(KV_HEADS):
            lanes = slice(head * HEAD_DIM, (head + 1) * HEAD_DIM)
            for block in range(blocks):
                place = slice(block * BLK_TOKENS, (block + 1) * BLK_TOKENS)
                key = staged[part, place, lanes].astype(jnp.float32)
                ready[part, head, place, 0:HEAD_DIM] = jnp.where(live[block], key, MARK).astype(
                    jnp.bfloat16
                )
            lanes = slice(WIDTH + head * HEAD_DIM, WIDTH + (head + 1) * HEAD_DIM)
            ready[part, head, :, HEAD_DIM:] = staged[part, :, lanes]
            send(part, head).start()
    for part in range(PACK_PARTS):
        for head in range(KV_HEADS):
            send(part, head).wait()


def pack(block_fill, cache_pool):
    span = PIECE_ROWS // PACK_PARTS
    hbm = pl.BlockSpec(memory_space=pltpu.HBM)
    return pl.pallas_call(
        pack_kernel,
        out_shape=jax.ShapeDtypeStruct((KV_HEADS, PIECE_ROWS, 2 * HEAD_DIM), jnp.bfloat16),
        in_specs=[pl.BlockSpec(memory_space=pltpu.SMEM), hbm],
        out_specs=hbm,
        scratch_shapes=[
            pltpu.VMEM((PACK_PARTS, span, 2 * WIDTH), jnp.bfloat16),
            pltpu.VMEM((PACK_PARTS, KV_HEADS, span, 2 * HEAD_DIM), jnp.bfloat16),
            pltpu.SemaphoreType.DMA((PACK_PARTS,)),
            pltpu.SemaphoreType.DMA((PACK_PARTS * KV_HEADS,)),
        ],
        compiler_params=pltpu.CompilerParams(vmem_limit_bytes=60 * 1024 * 1024),
        name="pack",
    )(block_fill, cache_pool.reshape(PIECE_ROWS, 2 * WIDTH))


def attend_kernel(codes, counts, group, kv, query, barred, out, keys, values, peaks, sums):
    values[:, :, HEAD_DIM:] = jnp.ones((TOGETHER, TOKENS, HEAD_DIM), jnp.bfloat16)
    row_rollout = lax.broadcasted_iota(jnp.int32, (ROWS, HEAD_DIM), 0) // GROUP
    lane = lax.broadcasted_iota(jnp.int32, (ROWS, HEAD_DIM), 1)

    def member_lanes(parity):
        mine = row_rollout + TILE * parity == lane
        return jnp.where(mine, 1.0, 0.0).astype(jnp.bfloat16)

    members = [member_lanes(parity) for parity in range(2)]
    pick = lax.broadcasted_iota(jnp.int32, (8, HEAD_DIM), 0)
    pick_lane = lax.broadcasted_iota(jnp.int32, (8, HEAD_DIM), 1)
    picked = jnp.where(pick == pick_lane, 1.0, 0.0).astype(jnp.bfloat16)

    def chunk_scores(tile, chunk, lane_of, size=CHUNK, member=None):
        member = member_lanes(tile & 1) if member is None else member
        rows = query[pl.ds(pl.multiple_of(tile * ROWS, ROWS), ROWS), :]
        left = jnp.concatenate([rows, member], axis=1)
        for slot in range(size):
            number = chunk * CHUNK + slot
            code = codes[tile, number]
            row = pl.multiple_of(code * BLK_TOKENS, BLK_TOKENS)
            place = pl.ds(slot * BLK_TOKENS, BLK_TOKENS)
            key = kv[pl.ds(row, BLK_TOKENS), 0:HEAD_DIM].astype(jnp.float32)
            live = (key < MARK) & (number < counts[0, tile])
            keys[lane_of, place, 0:HEAD_DIM] = jnp.where(live, key, 0.0).astype(jnp.bfloat16)
            keys[lane_of, place, HEAD_DIM:] = jnp.where(
                live, barred[pl.ds((tile >> 1) * BLOCKS + code, 1), :], DEAD
            ).astype(jnp.bfloat16)
            values[lane_of, place, 0:HEAD_DIM] = kv[pl.ds(row, BLK_TOKENS), HEAD_DIM:]
        return lax.dot_general(
            left,
            keys[lane_of, 0 : size * BLK_TOKENS],
            (((1,), (1,)), ((), ())),
            preferred_element_type=jnp.float32,
        )

    def highest(found, low):
        peak = jnp.maximum(jnp.max(found, axis=1, keepdims=True) * SCALE2, low)
        return peak.astype(jnp.bfloat16).astype(jnp.float32)

    def summed(found, peak, lane_of):
        weights = jnp.exp2(found * SCALE2 - peak).astype(jnp.bfloat16)
        return jnp.dot(
            weights, values[lane_of, 0 : found.shape[1]], preferred_element_type=jnp.float32
        )

    def put_out(tile, peak, sums):
        total = sums[:, HEAD_DIM:]
        coarse = total.astype(jnp.bfloat16).astype(jnp.float32)
        stats = jnp.where(lane == 0, peak, jnp.where(lane == 1, coarse, total - coarse))
        flat = lax.dot_general(
            picked,
            stats.astype(jnp.bfloat16),
            (((1,), (1,)), ((), ())),
            preferred_element_type=jnp.float32,
        )
        for part in range(TILE // 32):
            count = 32 * GROUP
            owner = tile * (TILE // 32) + part
            owner = (((group[0] >> 2) - (owner >> 2)) & 3) * 4 + ((group[0] - owner) & 3)
            out[owner, 0:count, :] = sums[
                part * count : (part + 1) * count, 0:HEAD_DIM
            ].astype(jnp.bfloat16)
            both = jnp.concatenate(
                [
                    flat[:, part * count : part * count + HEAD_DIM],
                    flat[:, part * count + HEAD_DIM : (part + 1) * count],
                ],
                axis=0,
            )
            out[owner, count:, :] = both.astype(jnp.bfloat16)

    def long_tile(tile):
        chunks = (counts[0, tile] + CHUNK - 1) // CHUNK
        found = chunk_scores(tile, 0, 0)
        peak = highest(found, LOW)
        peaks[...] = jnp.broadcast_to(peak, (ROWS, HEAD_DIM))
        sums[...] = summed(found, peak, 0)

        def more(chunk, _):
            found = chunk_scores(tile, chunk, 0)
            old = peaks[:, 0:1]
            peak = highest(found, old)
            sums[...] = sums[...] * jnp.exp2(old - peak) + summed(found, peak, 0)
            peaks[...] = jnp.broadcast_to(peak, (ROWS, HEAD_DIM))
            return 0

        lax.fori_loop(1, chunks, more, 0)
        put_out(tile, peaks[...], sums[...])

    def some_tiles(step, _):
        tiles = [step * TOGETHER + k for k in range(TOGETHER)]
        most = counts[0, tiles[0]]
        for tile in tiles[1:]:
            most = jnp.maximum(most, counts[0, tile])

        for fewer, size in zip((-1,) + SIZES, SIZES):

            @pl.when((most > fewer) & (most <= size))
            def _():
                found = [
                    chunk_scores(tile, 0, k, size, members[k % 2]) for k, tile in enumerate(tiles)
                ]
                peak = [highest(one, LOW) for one in found]
                added = [summed(found[k], peak[k], k) for k in range(TOGETHER)]
                for k, tile in enumerate(tiles):
                    put_out(tile, peak[k], added[k])

        @pl.when(most > CHUNK)
        def _():
            lax.fori_loop(0, TOGETHER, lambda k, _: long_tile(tiles[0] + k) or 0, 0)

        return 0

    lax.fori_loop(0, codes.shape[0] // TOGETHER, some_tiles, 0)


def attend(codes, counts, group, kv, query, barred):
    vmem = pl.BlockSpec(memory_space=pltpu.VMEM)
    smem = pl.BlockSpec(memory_space=pltpu.SMEM)
    sources = query.shape[0] // (32 * GROUP)
    return pl.pallas_call(
        attend_kernel,
        out_shape=jax.ShapeDtypeStruct((sources, OUT_ROWS, HEAD_DIM), jnp.bfloat16),
        in_specs=[smem, smem, smem, vmem, vmem, vmem],
        out_specs=vmem,
        scratch_shapes=[
            pltpu.VMEM((TOGETHER, TOKENS, 2 * HEAD_DIM), jnp.bfloat16),
            pltpu.VMEM((TOGETHER, TOKENS, 2 * HEAD_DIM), jnp.bfloat16),
            pltpu.VMEM((ROWS, HEAD_DIM), jnp.float32),
            pltpu.VMEM((ROWS, 2 * HEAD_DIM), jnp.float32),
        ],
        compiler_params=pltpu.CompilerParams(vmem_limit_bytes=26 * 1024 * 1024),
        cost_estimate=pl.CostEstimate(
            flops=4 * 4096 * 512 * 256, bytes_accessed=6 << 20, transcendentals=4096 * 512
        ),
        name="attend",
    )(codes, counts, group, kv, query, barred)


def finish_kernel(parts, query, entry, out, peaks, totals, ended):
    sources = parts.shape[0]
    count = parts.shape[1] - 16
    which = lax.broadcasted_iota(jnp.int32, (8, 2 * HEAD_DIM), 0)
    lane = lax.broadcasted_iota(jnp.int32, (8, 2 * HEAD_DIM), 1)
    spread = jnp.where(
        lane < HEAD_DIM, jnp.where(which == 0, 1.0, 0.0), jnp.where((which == 1) | (which == 2), 1.0, 0.0)
    ).astype(jnp.bfloat16)
    rollouts = count // GROUP
    own_key = jnp.broadcast_to(
        entry[:, 0:HEAD_DIM].astype(jnp.float32)[:, None, :], (rollouts, GROUP, HEAD_DIM)
    ).reshape(count, HEAD_DIM)
    own_value = jnp.broadcast_to(
        entry[:, HEAD_DIM:].astype(jnp.float32)[:, None, :], (rollouts, GROUP, HEAD_DIM)
    ).reshape(count, HEAD_DIM)
    own = jnp.sum(query[...].astype(jnp.float32) * own_key, axis=1, keepdims=True) * SCALE2
    highest = jnp.broadcast_to(own, (count, HEAD_DIM))
    for source in range(sources):
        flat = parts[source, count:, :].astype(jnp.float32)
        for half in range(count // HEAD_DIM):
            wide = lax.dot_general(
                flat[half * 8 : half * 8 + 8, :].astype(jnp.bfloat16),
                spread,
                (((0,), (0,)), ((), ())),
                preferred_element_type=jnp.float32,
            )
            place = pl.ds(half * HEAD_DIM, HEAD_DIM)
            peaks[source, place, :] = wide[:, :HEAD_DIM]
            totals[source, place, :] = wide[:, HEAD_DIM:]
        highest = jnp.maximum(highest, peaks[source])
    weight = jnp.exp2(own - highest)
    total = weight
    accum = weight * own_value
    for source in range(sources):
        weight = jnp.exp2(peaks[source] - highest)
        total = total + weight * totals[source]
        accum = accum + weight * parts[source, 0:count, :].astype(jnp.float32)
    ended[...] = accum / total
    for head in range(GROUP):
        out[:, head * HEAD_DIM : (head + 1) * HEAD_DIM] = ended[
            pl.ds(head, rollouts, stride=GROUP), :
        ].astype(jnp.bfloat16)


def finish(parts, query, entry):
    count = query.shape[0]
    vmem = pl.BlockSpec(memory_space=pltpu.VMEM)
    return pl.pallas_call(
        finish_kernel,
        out_shape=jax.ShapeDtypeStruct((count // GROUP, WIDTH), jnp.bfloat16),
        in_specs=[vmem, vmem, vmem],
        out_specs=vmem,
        scratch_shapes=[
            pltpu.VMEM((parts.shape[0], count, HEAD_DIM), jnp.float32),
            pltpu.VMEM((parts.shape[0], count, HEAD_DIM), jnp.float32),
            pltpu.VMEM((count, HEAD_DIM), jnp.float32),
        ],
        compiler_params=pltpu.CompilerParams(vmem_limit_bytes=50 * 1024 * 1024),
        name="finish",
    )(parts, query, entry)


def place_kernel(node, *refs):
    heads, out = refs[:-1], refs[-1]
    chips = len(heads) // 2
    for which in range(2):
        core = lax.rem(node[0] + which, 2)
        for hop, ref in zip((0, 3, 1, 2), heads[which * chips : (which + 1) * chips]):
            chip = lax.rem(node[0] // 2 - hop + chips, chips)
            start = pl.multiple_of((chip * 2 + core) * WIDTH, WIDTH)
            out[:, pl.ds(start, WIDTH)] = ref[...]


def place_heads(node, mine, other):
    vmem = pl.BlockSpec(memory_space=pltpu.VMEM)
    rollouts = mine[0].shape[0]
    return pl.pallas_call(
        place_kernel,
        out_shape=jax.ShapeDtypeStruct((rollouts, HEADS * HEAD_DIM), jnp.bfloat16),
        in_specs=[pl.BlockSpec(memory_space=pltpu.SMEM)] + [vmem] * (2 * len(mine)),
        out_specs=vmem,
        compiler_params=pltpu.CompilerParams(vmem_limit_bytes=16 * 1024 * 1024),
        name="place_heads",
    )(node.reshape(1).astype(jnp.int32), *mine, *other)


def visits_kernel(column, told, root, codes, counts, barred, hits, places):
    entries = LIST - ROOT_BLOCKS
    entry = lax.broadcasted_iota(jnp.int32, (2 * entries, HEAD_DIM), 0)
    lane = lax.broadcasted_iota(jnp.int32, (2 * entries, HEAD_DIM), 1)
    picked = jnp.where(entry == lane, 1.0, 0.0).astype(jnp.bfloat16)
    dims = (((1,), (1,)), ((), ()))
    turned = lax.dot_general(picked, told[...], dims, preferred_element_type=jnp.float32)
    turned = turned.astype(jnp.int32)

    def local(device, place):
        here = ((device & 15) == column[0]) & (device < NOBODY)
        return jnp.where(here, (device >> 4) * OWN_BLOCKS + place, -1)

    listed = local(turned[0:entries], turned[entries:])
    root_row = local(root[0:1, :], root[1:2, :])
    span = 64
    for part in range(BLOCKS // span):
        rows = slice(part * span, (part + 1) * span)
        number = lax.broadcasted_iota(jnp.int32, (span, HEAD_DIM), 0) + part * span
        lane = lax.broadcasted_iota(jnp.int32, (span, HEAD_DIM), 1)
        everyone = jnp.max(jnp.where(root_row == number, 1.0, 0.0), axis=1, keepdims=True)
        found = jnp.zeros((span, HEAD_DIM), jnp.float32)
        for pair in range(told.shape[0] // HEAD_DIM):
            member = jnp.broadcast_to(everyone, (span, HEAD_DIM))
            for index in range(entries):
                row = listed[index : index + 1, pair * HEAD_DIM : (pair + 1) * HEAD_DIM]
                member = jnp.where(row == number, 1.0, member)
            barred[pl.ds(pair * BLOCKS + part * span, span), :] = jnp.where(
                member > 0.5, 0.0, DEAD
            )
            for parity in range(2):
                mine = (lane < TILE) if parity == 0 else (lane >= TILE)
                hit = jnp.max(jnp.where(mine, member, 0.0), axis=1, keepdims=True)
                found = jnp.where(lane == 2 * pair + parity, hit, found)
        hits[rows, :] = found
    hit = hits[...]
    counts[...] = jnp.broadcast_to(jnp.sum(hit, axis=0, keepdims=True), counts.shape).astype(
        jnp.int32
    )
    row = lax.broadcasted_iota(jnp.int32, (BLOCKS, BLOCKS), 0)
    col = lax.broadcasted_iota(jnp.int32, (BLOCKS, BLOCKS), 1)
    before = jnp.where(col < row, 1.0, 0.0).astype(jnp.bfloat16)
    place = jnp.dot(before, hit.astype(jnp.bfloat16), preferred_element_type=jnp.float32)
    places[...] = jnp.where(hit > 0.5, place, -1.0)
    most = jnp.max(jnp.sum(hit, axis=0, keepdims=True))

    def listing(width):
        wide = lax.broadcasted_iota(jnp.int32, (BLOCKS, width), 1).astype(jnp.float32)
        number = lax.broadcasted_iota(jnp.int32, (BLOCKS, width), 0)
        for tile in range(codes.shape[0]):
            there = places[:, tile : tile + 1] == wide
            found = jnp.sum(jnp.where(there, number, 0), axis=0, keepdims=True)
            codes[tile : tile + 1, 0:width] = found

    @pl.when(most <= HEAD_DIM)
    def _():
        listing(HEAD_DIM)
        codes[:, HEAD_DIM:] = jnp.zeros((codes.shape[0], BLOCKS - HEAD_DIM), jnp.int32)

    @pl.when(most > HEAD_DIM)
    def _():
        listing(BLOCKS)


def visits(column, told, root):
    tiles = told.shape[0] // TILE
    vmem = pl.BlockSpec(memory_space=pltpu.VMEM)
    return pl.pallas_call(
        visits_kernel,
        out_shape=[
            jax.ShapeDtypeStruct((tiles, BLOCKS), jnp.int32),
            jax.ShapeDtypeStruct((8, HEAD_DIM), jnp.int32),
            jax.ShapeDtypeStruct((tiles // 2 * BLOCKS, HEAD_DIM), jnp.float32),
        ],
        in_specs=[pl.BlockSpec(memory_space=pltpu.SMEM), vmem, vmem],
        out_specs=[vmem] * 3,
        scratch_shapes=[
            pltpu.VMEM((BLOCKS, HEAD_DIM), jnp.float32),
            pltpu.VMEM((BLOCKS, HEAD_DIM), jnp.float32),
        ],
        compiler_params=pltpu.CompilerParams(vmem_limit_bytes=26 * 1024 * 1024),
        cost_estimate=pl.CostEstimate(flops=10**8, bytes_accessed=2 << 20, transcendentals=0),
        name="visits",
    )(column, told, root)


def per_device(queries, new_entry, block_lists, list_lengths, block_fill, cache_pool):
    node = lax.axis_index("node")
    column = lax.axis_index("group")
    groups = lax.axis_size("group")
    own_rows = queries.shape[0]

    sent = pack(block_fill, cache_pool)
    kv = lax.all_to_all(sent, "node", split_axis=0, concat_axis=0, tiled=True)
    kv = kv.reshape(HOLDERS * PIECE_ROWS, 2 * HEAD_DIM)

    head_query = lax.dynamic_slice_in_dim(queries, node * WIDTH, WIDTH, axis=1)
    entries = jnp.arange(LIST, dtype=jnp.int32)[None, :]
    listed = entries < list_lengths[:, None]
    device = jnp.where(listed, block_lists // OWN_BLOCKS, NOBODY)[:, ROOT_BLOCKS:]
    place = (block_lists % OWN_BLOCKS)[:, ROOT_BLOCKS:]
    coded = jnp.concatenate([device, place], axis=1).astype(jnp.bfloat16)
    coded = jnp.pad(coded, ((0, 0), (0, HEAD_DIM - coded.shape[1])))
    told = jnp.concatenate([head_query, coded], axis=1)
    sent, told = lax.optimization_barrier((sent, told))
    side = 4
    def shifted(value, hop_x, hop_z):
        pairs = [
            (x * side + z, (x + hop_x) % side * side + (z + hop_z) % side)
            for x in range(side)
            for z in range(side)
        ]
        return lax.ppermute(value, "group", pairs)

    line = jnp.stack([told] + [shifted(told, 0, hop) for hop in range(1, side)])
    told = jnp.stack([line] + [shifted(line, hop, 0) for hop in range(1, side)])
    told = told.reshape((groups,) + told.shape[2:])
    all_query = told[:, :, :WIDTH].reshape(groups * own_rows * GROUP, HEAD_DIM)
    coded = told[:, :, WIDTH:].reshape(groups * own_rows, HEAD_DIM)
    root = block_lists[0, :ROOT_BLOCKS]
    root = jnp.stack([root // OWN_BLOCKS, root % OWN_BLOCKS])
    root = jnp.pad(root, ((0, 6), (0, HEAD_DIM - ROOT_BLOCKS)), constant_values=NOBODY)
    group = column.reshape(1).astype(jnp.int32)
    codes, counts, barred = visits(group, coded, root)
    partial = attend(codes, counts, group, kv, all_query, barred)
    parts = lax.all_to_all(partial, "group", split_axis=0, concat_axis=0, tiled=True)
    key = lax.dynamic_slice_in_dim(new_entry, node * HEAD_DIM, HEAD_DIM, axis=1)
    value = lax.dynamic_slice_in_dim(new_entry, WIDTH + node * HEAD_DIM, HEAD_DIM, axis=1)
    done = finish(
        parts,
        head_query.reshape(own_rows * GROUP, HEAD_DIM),
        jnp.concatenate([key, value], axis=1),
    )
    nodes = lax.axis_size("node")

    def from_node(value, to):
        return lax.ppermute(value, "node", [(i, to(i)) for i in range(nodes)])

    def along(hop):
        return lambda i: (i + 2 * hop) % nodes

    mine = [done] + [from_node(done, along(hop)) for hop in (3, 1, 2)]
    other = [from_node(value, lambda i: i ^ 1) for value in mine]
    return place_heads(node, mine, other)


def solution(mesh):
    return jax.shard_map(
        per_device,
        mesh=mesh,
        in_specs=(
            P("group", None),
            P("group", None),
            P("group", None),
            P("group"),
            P(("node", "group")),
            P(("node", "group"), None, None),
        ),
        out_specs=P("group", None),
        check_vma=False,
    )
```

```python
import functools
import math

import jax
import jax.numpy as jnp
from jax import lax
from jax.experimental import pallas as pl
from jax.experimental.pallas import tpu as pltpu
from jax.sharding import PartitionSpec as P

HEADS = 64
KV_HEADS = 8
HEAD_DIM = 128
BLK_TOKENS = 16
ROOT_BLOCKS = 40
LIST = 64
WIDTH = KV_HEADS * HEAD_DIM
GROUP = HEADS // KV_HEADS
SCALE = 1.0 / math.sqrt(HEAD_DIM)
SCALE2 = SCALE * math.log2(math.e)

HOLDERS = 8
OWN_BLOCKS = 48
BLOCKS = HOLDERS * OWN_BLOCKS
PIECE_ROWS = OWN_BLOCKS * BLK_TOKENS
MARK = 2.0**120
TILE = 64
CHUNK = 40
SIZES = (24, 32, 40)
ROWS = TILE * GROUP
PACK_PARTS = 4
TOGETHER = 4
TOKENS = CHUNK * BLK_TOKENS
OUT_ROWS = 32 * GROUP + 16
LOW = -1e9
DEAD = -1e30
NOBODY = 255


def pack_kernel(fill, pool, out, staged, ready, arrived, left):
    span = PIECE_ROWS // PACK_PARTS

    def fetch(part):
        place = pl.ds(part * span, span)
        return pltpu.make_async_copy(pool.at[place, :], staged.at[part], arrived.at[part])

    def send(part, head):
        return pltpu.make_async_copy(
            ready.at[part, head],
            out.at[head, pl.ds(part * span, span), :],
            left.at[part * KV_HEADS + head],
        )

    for part in range(PACK_PARTS):
        fetch(part).start()
    token = lax.broadcasted_iota(jnp.int32, (BLK_TOKENS, HEAD_DIM), 0)
    blocks = span // BLK_TOKENS
    for part in range(PACK_PARTS):
        fetch(part).wait()
        live = [token < fill[part * blocks + block] for block in range(blocks)]
        for head in range(KV_HEADS):
            lanes = slice(head * HEAD_DIM, (head + 1) * HEAD_DIM)
            for block in range(blocks):
                place = slice(block * BLK_TOKENS, (block + 1) * BLK_TOKENS)
                key = staged[part, place, lanes].astype(jnp.float32)
                ready[part, head, place, 0:HEAD_DIM] = jnp.where(live[block], key, MARK).astype(
                    jnp.bfloat16
                )
            lanes = slice(WIDTH + head * HEAD_DIM, WIDTH + (head + 1) * HEAD_DIM)
            ready[part, head, :, HEAD_DIM:] = staged[part, :, lanes]
            send(part, head).start()
    for part in range(PACK_PARTS):
        for head in range(KV_HEADS):
            send(part, head).wait()


def pack(block_fill, cache_pool):
    span = PIECE_ROWS // PACK_PARTS
    hbm = pl.BlockSpec(memory_space=pltpu.HBM)
    return pl.pallas_call(
        pack_kernel,
        out_shape=jax.ShapeDtypeStruct((KV_HEADS, PIECE_ROWS, 2 * HEAD_DIM), jnp.bfloat16),
        in_specs=[pl.BlockSpec(memory_space=pltpu.SMEM), hbm],
        out_specs=hbm,
        scratch_shapes=[
            pltpu.VMEM((PACK_PARTS, span, 2 * WIDTH), jnp.bfloat16),
            pltpu.VMEM((PACK_PARTS, KV_HEADS, span, 2 * HEAD_DIM), jnp.bfloat16),
            pltpu.SemaphoreType.DMA((PACK_PARTS,)),
            pltpu.SemaphoreType.DMA((PACK_PARTS * KV_HEADS,)),
        ],
        compiler_params=pltpu.CompilerParams(vmem_limit_bytes=60 * 1024 * 1024),
        name="pack",
    )(block_fill, cache_pool.reshape(PIECE_ROWS, 2 * WIDTH))


def attend_kernel(codes, counts, group, kv, query, barred, out, keys, values, peaks, sums):
    values[:, :, HEAD_DIM:] = jnp.ones((TOGETHER, TOKENS, HEAD_DIM), jnp.bfloat16)
    row_rollout = lax.broadcasted_iota(jnp.int32, (ROWS, HEAD_DIM), 0) // GROUP
    lane = lax.broadcasted_iota(jnp.int32, (ROWS, HEAD_DIM), 1)

    def member_lanes(parity):
        mine = row_rollout + TILE * parity == lane
        return jnp.where(mine, 1.0, 0.0).astype(jnp.bfloat16)

    members = [member_lanes(parity) for parity in range(2)]
    pick = lax.broadcasted_iota(jnp.int32, (8, HEAD_DIM), 0)
    pick_lane = lax.broadcasted_iota(jnp.int32, (8, HEAD_DIM), 1)
    picked = jnp.where(pick == pick_lane, 1.0, 0.0).astype(jnp.bfloat16)

    def chunk_scores(tile, chunk, lane_of, size=CHUNK, member=None):
        member = member_lanes(tile & 1) if member is None else member
        rows = query[pl.ds(pl.multiple_of(tile * ROWS, ROWS), ROWS), :]
        left = jnp.concatenate([rows, member], axis=1)
        for slot in range(size):
            number = chunk * CHUNK + slot
            code = codes[tile, number]
            row = pl.multiple_of(code * BLK_TOKENS, BLK_TOKENS)
            place = pl.ds(slot * BLK_TOKENS, BLK_TOKENS)
            key = kv[pl.ds(row, BLK_TOKENS), 0:HEAD_DIM].astype(jnp.float32)
            live = (key < MARK) & (number < counts[0, tile])
            keys[lane_of, place, 0:HEAD_DIM] = jnp.where(live, key, 0.0).astype(jnp.bfloat16)
            keys[lane_of, place, HEAD_DIM:] = jnp.where(
                live, barred[pl.ds((tile >> 1) * BLOCKS + code, 1), :], DEAD
            ).astype(jnp.bfloat16)
            values[lane_of, place, 0:HEAD_DIM] = kv[pl.ds(row, BLK_TOKENS), HEAD_DIM:]
        return lax.dot_general(
            left,
            keys[lane_of, 0 : size * BLK_TOKENS],
            (((1,), (1,)), ((), ())),
            preferred_element_type=jnp.float32,
        )

    def highest(found, low):
        peak = jnp.maximum(jnp.max(found, axis=1, keepdims=True) * SCALE2, low)
        return peak.astype(jnp.bfloat16).astype(jnp.float32)

    def summed(found, peak, lane_of):
        weights = jnp.exp2(found * SCALE2 - peak).astype(jnp.bfloat16)
        return jnp.dot(
            weights, values[lane_of, 0 : found.shape[1]], preferred_element_type=jnp.float32
        )

    def put_out(tile, peak, sums):
        total = sums[:, HEAD_DIM:]
        coarse = total.astype(jnp.bfloat16).astype(jnp.float32)
        stats = jnp.where(lane == 0, peak, jnp.where(lane == 1, coarse, total - coarse))
        flat = lax.dot_general(
            picked,
            stats.astype(jnp.bfloat16),
            (((1,), (1,)), ((), ())),
            preferred_element_type=jnp.float32,
        )
        for part in range(TILE // 32):
            count = 32 * GROUP
            owner = tile * (TILE // 32) + part
            owner = (((group[0] >> 2) - (owner >> 2)) & 3) * 4 + ((group[0] - owner) & 3)
            out[owner, 0:count, :] = sums[
                part * count : (part + 1) * count, 0:HEAD_DIM
            ].astype(jnp.bfloat16)
            both = jnp.concatenate(
                [
                    flat[:, part * count : part * count + HEAD_DIM],
                    flat[:, part * count + HEAD_DIM : (part + 1) * count],
                ],
                axis=0,
            )
            out[owner, count:, :] = both.astype(jnp.bfloat16)

    def long_tile(tile):
        chunks = (counts[0, tile] + CHUNK - 1) // CHUNK
        found = chunk_scores(tile, 0, 0)
        peak = highest(found, LOW)
        peaks[...] = jnp.broadcast_to(peak, (ROWS, HEAD_DIM))
        sums[...] = summed(found, peak, 0)

        def more(chunk, _):
            found = chunk_scores(tile, chunk, 0)
            old = peaks[:, 0:1]
            peak = highest(found, old)
            sums[...] = sums[...] * jnp.exp2(old - peak) + summed(found, peak, 0)
            peaks[...] = jnp.broadcast_to(peak, (ROWS, HEAD_DIM))
            return 0

        lax.fori_loop(1, chunks, more, 0)
        put_out(tile, peaks[...], sums[...])

    def some_tiles(step, _):
        tiles = [step * TOGETHER + k for k in range(TOGETHER)]
        most = counts[0, tiles[0]]
        for tile in tiles[1:]:
            most = jnp.maximum(most, counts[0, tile])

        for fewer, size in zip((-1,) + SIZES, SIZES):

            @pl.when((most > fewer) & (most <= size))
            def _():
                found = [
                    chunk_scores(tile, 0, k, size, members[k % 2]) for k, tile in enumerate(tiles)
                ]
                peak = [highest(one, LOW) for one in found]
                added = [summed(found[k], peak[k], k) for k in range(TOGETHER)]
                for k, tile in enumerate(tiles):
                    put_out(tile, peak[k], added[k])

        @pl.when(most > CHUNK)
        def _():
            lax.fori_loop(0, TOGETHER, lambda k, _: long_tile(tiles[0] + k) or 0, 0)

        return 0

    lax.fori_loop(0, codes.shape[0] // TOGETHER, some_tiles, 0)


def attend(codes, counts, group, kv, query, barred):
    vmem = pl.BlockSpec(memory_space=pltpu.VMEM)
    smem = pl.BlockSpec(memory_space=pltpu.SMEM)
    sources = query.shape[0] // (32 * GROUP)
    return pl.pallas_call(
        attend_kernel,
        out_shape=jax.ShapeDtypeStruct((sources, OUT_ROWS, HEAD_DIM), jnp.bfloat16),
        in_specs=[smem, smem, smem, vmem, vmem, vmem],
        out_specs=vmem,
        scratch_shapes=[
            pltpu.VMEM((TOGETHER, TOKENS, 2 * HEAD_DIM), jnp.bfloat16),
            pltpu.VMEM((TOGETHER, TOKENS, 2 * HEAD_DIM), jnp.bfloat16),
            pltpu.VMEM((ROWS, HEAD_DIM), jnp.float32),
            pltpu.VMEM((ROWS, 2 * HEAD_DIM), jnp.float32),
        ],
        compiler_params=pltpu.CompilerParams(vmem_limit_bytes=26 * 1024 * 1024),
        cost_estimate=pl.CostEstimate(
            flops=4 * 4096 * 512 * 256, bytes_accessed=6 << 20, transcendentals=4096 * 512
        ),
        name="attend",
    )(codes, counts, group, kv, query, barred)


def finish_kernel(parts, query, entry, out, peaks, totals, ended):
    sources = parts.shape[0]
    count = parts.shape[1] - 16
    which = lax.broadcasted_iota(jnp.int32, (8, 2 * HEAD_DIM), 0)
    lane = lax.broadcasted_iota(jnp.int32, (8, 2 * HEAD_DIM), 1)
    spread = jnp.where(
        lane < HEAD_DIM, jnp.where(which == 0, 1.0, 0.0), jnp.where((which == 1) | (which == 2), 1.0, 0.0)
    ).astype(jnp.bfloat16)
    rollouts = count // GROUP
    own_key = jnp.broadcast_to(
        entry[:, 0:HEAD_DIM].astype(jnp.float32)[:, None, :], (rollouts, GROUP, HEAD_DIM)
    ).reshape(count, HEAD_DIM)
    own_value = jnp.broadcast_to(
        entry[:, HEAD_DIM:].astype(jnp.float32)[:, None, :], (rollouts, GROUP, HEAD_DIM)
    ).reshape(count, HEAD_DIM)
    own = jnp.sum(query[...].astype(jnp.float32) * own_key, axis=1, keepdims=True) * SCALE2
    highest = jnp.broadcast_to(own, (count, HEAD_DIM))
    for source in range(sources):
        flat = parts[source, count:, :].astype(jnp.float32)
        for half in range(count // HEAD_DIM):
            wide = lax.dot_general(
                flat[half * 8 : half * 8 + 8, :].astype(jnp.bfloat16),
                spread,
                (((0,), (0,)), ((), ())),
                preferred_element_type=jnp.float32,
            )
            place = pl.ds(half * HEAD_DIM, HEAD_DIM)
            peaks[source, place, :] = wide[:, :HEAD_DIM]
            totals[source, place, :] = wide[:, HEAD_DIM:]
        highest = jnp.maximum(highest, peaks[source])
    weight = jnp.exp2(own - highest)
    total = weight
    accum = weight * own_value
    for source in range(sources):
        weight = jnp.exp2(peaks[source] - highest)
        total = total + weight * totals[source]
        accum = accum + weight * parts[source, 0:count, :].astype(jnp.float32)
    ended[...] = accum / total
    for head in range(GROUP):
        out[:, head * HEAD_DIM : (head + 1) * HEAD_DIM] = ended[
            pl.ds(head, rollouts, stride=GROUP), :
        ].astype(jnp.bfloat16)


def finish(parts, query, entry):
    count = query.shape[0]
    vmem = pl.BlockSpec(memory_space=pltpu.VMEM)
    return pl.pallas_call(
        finish_kernel,
        out_shape=jax.ShapeDtypeStruct((count // GROUP, WIDTH), jnp.bfloat16),
        in_specs=[vmem, vmem, vmem],
        out_specs=vmem,
        scratch_shapes=[
            pltpu.VMEM((parts.shape[0], count, HEAD_DIM), jnp.float32),
            pltpu.VMEM((parts.shape[0], count, HEAD_DIM), jnp.float32),
            pltpu.VMEM((count, HEAD_DIM), jnp.float32),
        ],
        compiler_params=pltpu.CompilerParams(vmem_limit_bytes=50 * 1024 * 1024),
        name="finish",
    )(parts, query, entry)


def place_kernel(node, *refs):
    heads, out = refs[:-1], refs[-1]
    chips = len(heads) // 2
    for which in range(2):
        core = lax.rem(node[0] + which, 2)
        for hop, ref in zip((0, 3, 1, 2), heads[which * chips : (which + 1) * chips]):
            chip = lax.rem(node[0] // 2 - hop + chips, chips)
            start = pl.multiple_of((chip * 2 + core) * WIDTH, WIDTH)
            out[:, pl.ds(start, WIDTH)] = ref[...]


def place_heads(node, mine, other):
    vmem = pl.BlockSpec(memory_space=pltpu.VMEM)
    rollouts = mine[0].shape[0]
    return pl.pallas_call(
        place_kernel,
        out_shape=jax.ShapeDtypeStruct((rollouts, HEADS * HEAD_DIM), jnp.bfloat16),
        in_specs=[pl.BlockSpec(memory_space=pltpu.SMEM)] + [vmem] * (2 * len(mine)),
        out_specs=vmem,
        compiler_params=pltpu.CompilerParams(vmem_limit_bytes=16 * 1024 * 1024),
        name="place_heads",
    )(node.reshape(1).astype(jnp.int32), *mine, *other)


def visits_kernel(column, told, root, codes, counts, barred, hits, places):
    entries = LIST - ROOT_BLOCKS
    entry = lax.broadcasted_iota(jnp.int32, (2 * entries, HEAD_DIM), 0)
    lane = lax.broadcasted_iota(jnp.int32, (2 * entries, HEAD_DIM), 1)
    picked = jnp.where(entry == lane, 1.0, 0.0).astype(jnp.bfloat16)
    dims = (((1,), (1,)), ((), ()))
    turned = lax.dot_general(picked, told[...], dims, preferred_element_type=jnp.float32)
    turned = turned.astype(jnp.int32)

    def local(device, place):
        here = ((device & 15) == column[0]) & (device < NOBODY)
        return jnp.where(here, (device >> 4) * OWN_BLOCKS + place, -1)

    listed = local(turned[0:entries], turned[entries:])
    root_row = local(root[0:1, :], root[1:2, :])
    span = 64
    for part in range(BLOCKS // span):
        rows = slice(part * span, (part + 1) * span)
        number = lax.broadcasted_iota(jnp.int32, (span, HEAD_DIM), 0) + part * span
        lane = lax.broadcasted_iota(jnp.int32, (span, HEAD_DIM), 1)
        everyone = jnp.max(jnp.where(root_row == number, 1.0, 0.0), axis=1, keepdims=True)
        found = jnp.zeros((span, HEAD_DIM), jnp.float32)
        for pair in range(told.shape[0] // HEAD_DIM):
            member = jnp.broadcast_to(everyone, (span, HEAD_DIM))
            for index in range(entries):
                row = listed[index : index + 1, pair * HEAD_DIM : (pair + 1) * HEAD_DIM]
                member = jnp.where(row == number, 1.0, member)
            barred[pl.ds(pair * BLOCKS + part * span, span), :] = jnp.where(
                member > 0.5, 0.0, DEAD
            )
            for parity in range(2):
                mine = (lane < TILE) if parity == 0 else (lane >= TILE)
                hit = jnp.max(jnp.where(mine, member, 0.0), axis=1, keepdims=True)
                found = jnp.where(lane == 2 * pair + parity, hit, found)
        hits[rows, :] = found
    hit = hits[...]
    counts[...] = jnp.broadcast_to(jnp.sum(hit, axis=0, keepdims=True), counts.shape).astype(
        jnp.int32
    )
    row = lax.broadcasted_iota(jnp.int32, (BLOCKS, BLOCKS), 0)
    col = lax.broadcasted_iota(jnp.int32, (BLOCKS, BLOCKS), 1)
    before = jnp.where(col < row, 1.0, 0.0).astype(jnp.bfloat16)
    place = jnp.dot(before, hit.astype(jnp.bfloat16), preferred_element_type=jnp.float32)
    places[...] = jnp.where(hit > 0.5, place, -1.0)
    most = jnp.max(jnp.sum(hit, axis=0, keepdims=True))

    def listing(width):
        wide = lax.broadcasted_iota(jnp.int32, (BLOCKS, width), 1).astype(jnp.float32)
        number = lax.broadcasted_iota(jnp.int32, (BLOCKS, width), 0)
        for tile in range(codes.shape[0]):
            there = places[:, tile : tile + 1] == wide
            found = jnp.sum(jnp.where(there, number, 0), axis=0, keepdims=True)
            codes[tile : tile + 1, 0:width] = found

    @pl.when(most <= HEAD_DIM)
    def _():
        listing(HEAD_DIM)
        codes[:, HEAD_DIM:] = jnp.zeros((codes.shape[0], BLOCKS - HEAD_DIM), jnp.int32)

    @pl.when(most > HEAD_DIM)
    def _():
        listing(BLOCKS)


def visits(column, told, root):
    tiles = told.shape[0] // TILE
    vmem = pl.BlockSpec(memory_space=pltpu.VMEM)
    return pl.pallas_call(
        visits_kernel,
        out_shape=[
            jax.ShapeDtypeStruct((tiles, BLOCKS), jnp.int32),
            jax.ShapeDtypeStruct((8, HEAD_DIM), jnp.int32),
            jax.ShapeDtypeStruct((tiles // 2 * BLOCKS, HEAD_DIM), jnp.float32),
        ],
        in_specs=[pl.BlockSpec(memory_space=pltpu.SMEM), vmem, vmem],
        out_specs=[vmem] * 3,
        scratch_shapes=[
            pltpu.VMEM((BLOCKS, HEAD_DIM), jnp.float32),
            pltpu.VMEM((BLOCKS, HEAD_DIM), jnp.float32),
        ],
        compiler_params=pltpu.CompilerParams(vmem_limit_bytes=26 * 1024 * 1024),
        cost_estimate=pl.CostEstimate(flops=10**8, bytes_accessed=2 << 20, transcendentals=0),
        name="visits",
    )(column, told, root)


def per_device(queries, new_entry, block_lists, list_lengths, block_fill, cache_pool):
    node = lax.axis_index("node")
    column = lax.axis_index("group")
    groups = lax.axis_size("group")
    own_rows = queries.shape[0]

    sent = pack(block_fill, cache_pool)
    kv = lax.all_to_all(sent, "node", split_axis=0, concat_axis=0, tiled=True)
    kv = kv.reshape(HOLDERS * PIECE_ROWS, 2 * HEAD_DIM)

    head_query = lax.dynamic_slice_in_dim(queries, node * WIDTH, WIDTH, axis=1)
    entries = jnp.arange(LIST, dtype=jnp.int32)[None, :]
    listed = entries < list_lengths[:, None]
    device = jnp.where(listed, block_lists // OWN_BLOCKS, NOBODY)[:, ROOT_BLOCKS:]
    place = (block_lists % OWN_BLOCKS)[:, ROOT_BLOCKS:]
    coded = jnp.concatenate([device, place], axis=1).astype(jnp.bfloat16)
    coded = jnp.pad(coded, ((0, 0), (0, HEAD_DIM - coded.shape[1])))
    told = jnp.concatenate([head_query, coded], axis=1)
    sent, told = lax.optimization_barrier((sent, told))
    side = 4
    def shifted(value, hop_x, hop_z):
        pairs = [
            (x * side + z, (x + hop_x) % side * side + (z + hop_z) % side)
            for x in range(side)
            for z in range(side)
        ]
        return lax.ppermute(value, "group", pairs)

    along_z = {hop: shifted(told, 0, hop) for hop in (3, 1, 2)}
    line = jnp.stack([told] + [along_z[hop] for hop in range(1, side)])
    along_x = {hop: shifted(line, hop, 0) for hop in (3, 1, 2)}
    told = jnp.stack([line] + [along_x[hop] for hop in range(1, side)])
    told = told.reshape((groups,) + told.shape[2:])
    all_query = told[:, :, :WIDTH].reshape(groups * own_rows * GROUP, HEAD_DIM)
    coded = told[:, :, WIDTH:].reshape(groups * own_rows, HEAD_DIM)
    root = block_lists[0, :ROOT_BLOCKS]
    root = jnp.stack([root // OWN_BLOCKS, root % OWN_BLOCKS])
    root = jnp.pad(root, ((0, 6), (0, HEAD_DIM - ROOT_BLOCKS)), constant_values=NOBODY)
    group = column.reshape(1).astype(jnp.int32)
    codes, counts, barred = visits(group, coded, root)
    partial = attend(codes, counts, group, kv, all_query, barred)
    parts = lax.all_to_all(partial, "group", split_axis=0, concat_axis=0, tiled=True)
    key = lax.dynamic_slice_in_dim(new_entry, node * HEAD_DIM, HEAD_DIM, axis=1)
    value = lax.dynamic_slice_in_dim(new_entry, WIDTH + node * HEAD_DIM, HEAD_DIM, axis=1)
    done = finish(
        parts,
        head_query.reshape(own_rows * GROUP, HEAD_DIM),
        jnp.concatenate([key, value], axis=1),
    )
    nodes = lax.axis_size("node")

    def from_node(value, to):
        return lax.ppermute(value, "node", [(i, to(i)) for i in range(nodes)])

    def along(hop):
        return lambda i: (i + 2 * hop) % nodes

    mine = [done] + [from_node(done, along(hop)) for hop in (3, 1, 2)]
    other = [from_node(value, lambda i: i ^ 1) for value in mine]
    return place_heads(node, mine, other)


def solution(mesh):
    return jax.shard_map(
        per_device,
        mesh=mesh,
        in_specs=(
            P("group", None),
            P("group", None),
            P("group", None),
            P("group"),
            P(("node", "group")),
            P(("node", "group"), None, None),
        ),
        out_specs=P("group", None),
        check_vma=False,
    )
```
